32 devices in a mesh: col: 16 (over z, y, core), seq: 2 (over x).
Axes of the slice: x: 2, y: 2, z: 4, core: 2. Of those that a mesh axis runs over, the one named last changes fastest.
Arguments:
- history_items: int32 [16, 1024], P(None, 'seq'), may hold values from 0 to 65535
- lengths: int32 [16], replicated, may hold values from 64 to 1024, as said below
- item_table: float32 [512, 65536], P('col'), may hold values from -4 to 4
- input_weight: bfloat16 [512, 2048], replicated, may hold values from -0.25 to 0.25
- output_weight: bfloat16 [512, 512], replicated, may hold values from -0.25 to 0.25
- output_cotangent: bfloat16 [16, 1024, 512], P('col', 'seq'), may hold values from -6 to 6
Outputs:
- layer_output: bfloat16 [16, 1024, 512], P('col', 'seq')
- table_gradient: float32 [512, 65536], P('col', 'seq')
The draws below stay inside these ranges and needn't reach their ends.
Inputs may be any that keep to these rules, and one draw needn't show every extreme that they name: `lengths`: in every draw one history has exactly 1024 items.
All inputs are finite; a program needn't handle non-finite values.
Results may differ from the reference program's by a relative error of at most 0.0077.
Values may be sent and summed in bfloat16 or wider, within the bound.
A program may use at most 128 MiB of HBM per device.

```python
import math
import jax
import jax.numpy as jnp
import numpy as np
from jax import lax

D = 512
H = 8
DH = 64
LEN = 1024
TABLE_ROWS = 65536
USERS = 16


def draw_lengths(key, part):
    draw_key, pick_key = jax.random.split(key)
    drawn = jax.random.randint(draw_key, (USERS,), LEN // 16, LEN + 1, dtype=jnp.int32)
    longest = jax.random.randint(pick_key, (), 0, USERS, dtype=jnp.int32)
    return jnp.where(jnp.arange(USERS, dtype=jnp.int32) == longest, LEN, drawn).astype(jnp.int32)


def place_ends(values, stream_key, smallest, top_value):
    longest = values.shape.index(max(values.shape))
    spots = []
    for shift in (0, 1):
        where = [jax.random.randint(jax.random.fold_in(stream_key, axis), (), 0, length) for axis, length in enumerate(values.shape)]
        where[longest] = (where[longest] + shift) % values.shape[longest]
        spots.append(tuple(where))
    return values.at[spots[0]].set(smallest).at[spots[1]].set(top_value)


def shard_levels(stream_key, shape, cuts, least, high):
    level = 1.0
    for axis_at, blocks in cuts:
        heights = jax.random.uniform(jax.random.fold_in(jax.random.fold_in(stream_key, 6), axis_at), (blocks,), jnp.float32, least / len(cuts), high / len(cuts))
        level = level * jnp.repeat(jnp.exp(heights), shape[axis_at] // blocks).reshape((-1,) + (1,) * (len(shape) - 1 - axis_at))
    return level


def cumulative_ranks(number_of, slope):
    loads = [(1 << 20) // math.isqrt(standing ** slope) + 1 for standing in range(1, number_of + 1)]
    spread = 1 + sum(loads) // (1 << 30)
    return np.cumsum(np.array([max(1, weight // spread) for weight in loads]))


def skewed_ids(stream_key, shape, amount, skew):
    table = cumulative_ranks(amount, skew)
    pick = jax.random.randint(jax.random.fold_in(stream_key, 1), shape, 0, int(table[amount - 1]))
    standing = jnp.searchsorted(jnp.asarray(table, jnp.int32), pick, side="right")
    return jax.random.permutation(jax.random.fold_in(stream_key, 2), amount)[standing].astype(jnp.int32)


def centred(rng, shape, width, reach, cuts=(), held_as=jnp.bfloat16):
    result = jax.random.normal(rng, shape, jnp.float32) * width
    if len(cuts) > 0:
        result = shard_levels(rng, shape, cuts, -0.22, 0.18) * result
    return jnp.clip(result, min=-reach, max=reach).astype(held_as)


def setup_inputs(seed: int = 0) -> dict:
    seeds = jax.random.split(jax.random.key(seed), 7)
    return {
        "history_items": place_ends(skewed_ids(seeds[0], (USERS, LEN), TABLE_ROWS, 1), jax.random.fold_in(seeds[0], 3), 0, TABLE_ROWS - 1).astype(jnp.int32),
        "lengths": draw_lengths(jax.random.fold_in(seeds[6], 71), 0),
        "item_table": centred(seeds[2], (D, TABLE_ROWS), 0.5, 4.0, ((0, 16),), jnp.float32),
        "input_weight": centred(seeds[3], (D, 4 * H * DH), D ** -0.5, 0.25),
        "output_weight": centred(seeds[4], (H * DH, D), (H * DH) ** -0.5, 0.25),
        "output_cotangent": centred(seeds[5], (USERS, LEN, D), 1.0, 6.0, ((0, 16), (1, 2))),
    }


norm_epsilon = 1e-05

def layer_norm(inputs):
    average = lax.optimization_barrier(jnp.mean(inputs, axis=-1, keepdims=True))
    centered = inputs - average
    variance = lax.optimization_barrier(jnp.mean(centered * centered, axis=-1, keepdims=True))
    return centered * lax.rsqrt(variance + norm_epsilon)

def silu_slope(inputs):
    sigmoid_part = jax.nn.sigmoid(inputs)
    return sigmoid_part * (1.0 + inputs * (1.0 - sigmoid_part))

def one_user(item_table, input_weight, output_weight, item_row, length, grad_row):
    hidden = H * DH
    score_scale = DH ** (-0.5)
    length_scale = 1.0 / LEN
    looked = jnp.take(item_table, item_row, axis=1).T
    embedded = lax.optimization_barrier(looked.astype(jnp.bfloat16))
    features = embedded.astype(jnp.float32)
    normed = layer_norm(features).astype(jnp.bfloat16)
    preact = jnp.dot(normed, input_weight, preferred_element_type=jnp.float32)
    activated = jax.nn.silu(preact)
    update_part = activated[:, :hidden].astype(jnp.bfloat16)
    value_part = activated[:, hidden:2 * hidden].astype(jnp.bfloat16)
    query_part = activated[:, 2 * hidden:3 * hidden].astype(jnp.bfloat16)
    key_part = activated[:, 3 * hidden:].astype(jnp.bfloat16)
    query_heads = query_part.astype(jnp.float32).reshape(LEN, H, DH)
    key_heads = key_part.astype(jnp.float32).reshape(LEN, H, DH)
    value_heads = value_part.astype(jnp.float32).reshape(LEN, H, DH)
    positions = jnp.arange(LEN, dtype=jnp.int32)
    allowed = (positions[None, :] <= positions[:, None]) & (positions < length)[None, :]
    valid = positions < length
    scores = jnp.einsum('qhd,khd->hqk', query_heads, key_heads) * score_scale
    point_weights = jnp.where(allowed[None], jax.nn.silu(scores) * length_scale, 0.0).astype(jnp.bfloat16)
    attended = jnp.einsum('hqk,khd->qhd', point_weights.astype(jnp.float32), value_heads).reshape(LEN, hidden)
    normed_att = layer_norm(attended)
    gated = (normed_att * update_part.astype(jnp.float32)).astype(jnp.bfloat16)
    mixed = jnp.dot(gated, output_weight, preferred_element_type=jnp.float32) + features
    layer_output = jnp.where(valid[:, None], mixed, 0.0).astype(jnp.bfloat16)
    cotangent = jnp.where(valid[:, None], grad_row, jnp.zeros_like(grad_row))
    gated_grad = jnp.dot(cotangent, output_weight.T, preferred_element_type=jnp.float32)
    normed_grad = gated_grad * update_part.astype(jnp.float32)
    update_grad = gated_grad * normed_att
    attended_back = jax.vjp(layer_norm, attended)[1]
    attended_grad = attended_back(normed_grad)[0].astype(jnp.bfloat16)
    attended_heads = attended_grad.astype(jnp.float32).reshape(LEN, H, DH)
    weight_grad = jnp.einsum('qhd,khd->hqk', attended_heads, value_heads)
    score_grad = jnp.where(allowed[None], weight_grad * silu_slope(scores) * length_scale, 0.0).astype(jnp.bfloat16).astype(jnp.float32)
    query_grad = jnp.einsum('hqk,khd->qhd', score_grad, key_heads) * score_scale
    key_grad = jnp.einsum('hqk,qhd->khd', score_grad, query_heads) * score_scale
    value_grad = jnp.einsum('hqk,qhd->khd', point_weights.astype(jnp.float32), attended_heads)
    activation_grad = jnp.concatenate([update_grad, value_grad.reshape(LEN, hidden), query_grad.reshape(LEN, hidden), key_grad.reshape(LEN, hidden)], axis=-1)
    preact_grad = (activation_grad * silu_slope(preact)).astype(jnp.bfloat16)
    entry_grad = jnp.dot(preact_grad, input_weight.T, preferred_element_type=jnp.float32)
    features_back = jax.vjp(layer_norm, features)[1]
    input_grad = cotangent.astype(jnp.float32) + features_back(entry_grad)[0]
    return (layer_output, input_grad)

def reference(history_items, lengths, item_table, input_weight, output_weight, output_cotangent):

    def per_user(inputs):
        item_row, length, grad_row = inputs
        return one_user(item_table, input_weight, output_weight, item_row, length, grad_row)
    layer_output, input_grad = lax.map(per_user, (history_items, lengths, output_cotangent))
    table_gradient = jnp.zeros((D, TABLE_ROWS), jnp.float32).at[:, history_items.reshape(-1)].add(input_grad.reshape(-1, D).T)
    return (layer_output, table_gradient)
```

```python
import functools
import jax
import jax.numpy as jnp
from jax import lax
from jax.experimental import pallas as pl
from jax.experimental.pallas import tpu as pltpu
from jax.sharding import PartitionSpec as P

H = 8
DH = 64
LEN = 1024


norm_epsilon = 1e-05


def layer_norm(inputs):
    average = jnp.mean(inputs, axis=-1, keepdims=True)
    centered = inputs - average
    variance = jnp.mean(centered * centered, axis=-1, keepdims=True)
    return centered * lax.rsqrt(variance + norm_epsilon)


def silu_slope(inputs):
    sigmoid_part = jax.nn.sigmoid(inputs)
    return sigmoid_part * (1.0 + inputs * (1.0 - sigmoid_part))


LANES = 128
COPIES = 8
VMEM_BYTES = 58 * 1024 * 1024


def packed_place(items, feat):
    groups = LANES // feat
    row = (items // (LANES * groups)) * LANES + items % LANES
    slot = (items // LANES) % groups
    return row, slot


def lookup_kernel(rows_ref, slot_ref, table_ref, out_ref, packed, picked):
    feat, table_cols = table_ref.shape
    users, _, seq_rows = slot_ref.shape
    groups = LANES // feat
    span = LANES * groups

    def pack(block, carry):
        base = pl.multiple_of(block * span, span)
        parts = [table_ref[:, pl.ds(base + g * LANES, LANES)] for g in range(groups)]
        turned = jnp.concatenate(parts, axis=0).T
        packed[pl.ds(pl.multiple_of(block * LANES, LANES), LANES), :] = turned
        return carry

    lax.fori_loop(0, table_cols // span, pack, 0, unroll=2)

    def one_user(user, carry):
        def pick(step, inner):
            base = pl.multiple_of(step * 32, 32)
            for offset in range(32):
                row = rows_ref[user, base + offset]
                picked[pl.ds(base + offset, 1), :] = packed[pl.ds(row, 1), :]
            return inner

        lax.fori_loop(0, seq_rows // 32, pick, 0)
        for part in range(seq_rows // LANES):
            turned = picked[pl.ds(part * LANES, LANES), :].T
            slot = slot_ref[user, :, pl.ds(part * LANES, LANES)]
            total = jnp.zeros((feat, LANES), jnp.float32)
            for g in range(groups):
                total = jnp.where(slot == g, turned[g * feat : (g + 1) * feat, :], total)
            out_ref[user, :, pl.ds(part * LANES, LANES)] = total.astype(out_ref.dtype)
        return carry

    lax.fori_loop(0, users, one_user, 0)


def lookup(items, item_table):
    feat, table_cols = item_table.shape
    users, seq_rows = items.shape
    row, slot = packed_place(items, feat)
    return pl.pallas_call(
        lookup_kernel,
        out_shape=jax.ShapeDtypeStruct((users, feat, seq_rows), jnp.bfloat16),
        in_specs=[
            pl.BlockSpec(memory_space=pltpu.SMEM),
            pl.BlockSpec(memory_space=pltpu.VMEM),
            pl.BlockSpec(memory_space=pltpu.VMEM),
        ],
        out_specs=pl.BlockSpec(memory_space=pltpu.VMEM),
        scratch_shapes=[
            pltpu.VMEM((table_cols * feat // LANES, LANES), jnp.float32),
            pltpu.VMEM((seq_rows, LANES), jnp.float32),
        ],
        compiler_params=pltpu.CompilerParams(vmem_limit_bytes=VMEM_BYTES),
        name="lookup",
    )(row, slot[:, None], item_table)


def scatter_kernel(rows_ref, slot_ref, grad_ref, out_ref, placed, *sums):
    feat, owned = out_ref.shape
    blocks, _, seq_rows = slot_ref.shape
    groups = LANES // feat
    span = LANES * groups

    def clear(step, carry):
        at = pl.ds(pl.multiple_of(step * LANES, LANES), LANES)
        for total in sums:
            total[at, :] = jnp.zeros((LANES, LANES), jnp.float32)
        return carry

    lax.fori_loop(0, owned // span, clear, 0)

    def one_block(block, carry):
        for part in range(seq_rows // LANES):
            grad = grad_ref[block, :, pl.ds(part * LANES, LANES)].astype(jnp.float32)
            slot = slot_ref[block, :, pl.ds(part * LANES, LANES)]
            spread = jnp.concatenate(
                [jnp.where(slot == g, grad, 0.0) for g in range(groups)], axis=0
            )
            placed[pl.ds(part * LANES, LANES), :] = spread.T

        def add(step, inner):
            base = pl.multiple_of(step * 4 * COPIES, 4 * COPIES)
            for quarter in range(4):
                first = base + quarter * COPIES
                rows = [rows_ref[block, first + n] for n in range(COPIES)]
                news = [
                    sums[n][pl.ds(rows[n], 1), :] + placed[pl.ds(first + n, 1), :]
                    for n in range(COPIES)
                ]
                for n in range(COPIES):
                    sums[n][pl.ds(rows[n], 1), :] = news[n]
            return inner

        lax.fori_loop(0, seq_rows // (4 * COPIES), add, 0)
        return carry

    lax.fori_loop(0, blocks, one_block, 0)

    def unpack(step, carry):
        at = pl.ds(pl.multiple_of(step * LANES, LANES), LANES)
        total = sums[0][at, :]
        for other in sums[1:]:
            total = total + other[at, :]
        turned = total.T
        base = pl.multiple_of(step * span, span)
        for g in range(groups):
            out_ref[:, pl.ds(base + g * LANES, LANES)] = turned[g * feat : (g + 1) * feat, :]
        return carry

    lax.fori_loop(0, owned // span, unpack, 0, unroll=2)


def scatter(items, grads, owned, seq_index):
    feat = grads.shape[1]
    local = items % owned
    row, slot = packed_place(local, feat)
    slot = jnp.where(items // owned == seq_index, slot, -1)
    packed_rows = owned * feat // LANES
    return pl.pallas_call(
        scatter_kernel,
        out_shape=jax.ShapeDtypeStruct((feat, owned), jnp.float32),
        in_specs=[
            pl.BlockSpec(memory_space=pltpu.SMEM),
            pl.BlockSpec(memory_space=pltpu.VMEM),
            pl.BlockSpec(memory_space=pltpu.VMEM),
        ],
        out_specs=pl.BlockSpec(memory_space=pltpu.VMEM),
        scratch_shapes=[pltpu.VMEM((grads.shape[2], LANES), jnp.float32)]
        + [pltpu.VMEM((packed_rows, LANES), jnp.float32)] * COPIES,
        compiler_params=pltpu.CompilerParams(vmem_limit_bytes=VMEM_BYTES),
        name="scatter",
    )(row, slot[:, None], grads)


def per_device(history_items, lengths, item_table, input_weight, output_weight, output_cotangent):
    user_count = history_items.shape[0]
    seq_rows = history_items.shape[1]
    feat_cols = item_table.shape[0]
    hidden = H * DH
    score_scale = DH ** (-0.5)
    length_scale = 1.0 / LEN
    col_index = lax.axis_index("col")
    seq_index = lax.axis_index("seq")
    chosen = jnp.arange(lengths.shape[0], dtype=jnp.int32) == col_index
    length = jnp.sum(jnp.where(chosen, lengths, 0))
    every_item = lax.all_gather(history_items, "seq", axis=0, tiled=True)
    looked = lookup(history_items, item_table)
    embedded = lax.all_to_all(looked, "col", split_axis=0, concat_axis=1, tiled=True)[0].T
    features = embedded.astype(jnp.float32)
    normed = layer_norm(features).astype(jnp.bfloat16)
    preact = jnp.dot(normed, input_weight, preferred_element_type=jnp.float32)
    activated = jax.nn.silu(preact)
    update_part = activated[:, :hidden].astype(jnp.bfloat16)
    value_heads = activated[:, hidden : 2 * hidden].astype(jnp.bfloat16).reshape(seq_rows, H, DH)
    query_heads = (
        activated[:, 2 * hidden : 3 * hidden].astype(jnp.bfloat16).reshape(seq_rows, H, DH)
    )
    key_heads = activated[:, 3 * hidden :].astype(jnp.bfloat16).reshape(seq_rows, H, DH)
    positions = seq_index * seq_rows + jnp.arange(seq_rows, dtype=jnp.int32)
    valid = positions < length
    keys_in = lax.all_gather(key_heads, "seq", axis=0, tiled=True)
    values_in = lax.all_gather(value_heads, "seq", axis=0, tiled=True)
    remote_pos = jnp.arange(keys_in.shape[0], dtype=jnp.int32)
    allowed = (remote_pos[None, :] <= positions[:, None]) & (remote_pos < length)[None, :]
    scores = (
        jnp.einsum("qhd,khd->hqk", query_heads, keys_in, preferred_element_type=jnp.float32)
        * score_scale
    )
    point_weights = jnp.where(allowed[None], jax.nn.silu(scores) * length_scale, 0.0).astype(
        jnp.bfloat16
    )
    attended = jnp.einsum(
        "hqk,khd->qhd", point_weights, values_in, preferred_element_type=jnp.float32
    ).reshape(seq_rows, hidden)
    normed_att = layer_norm(attended)
    gated = (normed_att * update_part.astype(jnp.float32)).astype(jnp.bfloat16)
    mixed = jnp.dot(gated, output_weight, preferred_element_type=jnp.float32) + features
    layer_output = jnp.where(valid[:, None], mixed, 0.0).astype(jnp.bfloat16)
    grad_row = output_cotangent[0]
    cotangent = jnp.where(valid[:, None], grad_row, jnp.zeros_like(grad_row))
    gated_grad = jnp.dot(cotangent, output_weight.T, preferred_element_type=jnp.float32)
    normed_grad = gated_grad * update_part.astype(jnp.float32)
    update_grad = gated_grad * normed_att
    attended_back = jax.vjp(layer_norm, attended)[1]
    attended_heads = attended_back(normed_grad)[0].astype(jnp.bfloat16).reshape(seq_rows, H, DH)
    keys_in = lax.all_gather(key_heads, "seq", axis=0, tiled=True)
    values_in = lax.all_gather(value_heads, "seq", axis=0, tiled=True)
    queries_in = lax.all_gather(query_heads, "seq", axis=0, tiled=True)
    attended_in = lax.all_gather(attended_heads, "seq", axis=0, tiled=True)
    remote_pos = jnp.arange(keys_in.shape[0], dtype=jnp.int32)
    allowed = (remote_pos[None, :] <= positions[:, None]) & (remote_pos < length)[None, :]
    scores = (
        jnp.einsum("qhd,khd->hqk", query_heads, keys_in, preferred_element_type=jnp.float32)
        * score_scale
    )
    weight_grad = jnp.einsum(
        "qhd,khd->hqk", attended_heads, values_in, preferred_element_type=jnp.float32
    )
    score_grad = jnp.where(
        allowed[None], weight_grad * silu_slope(scores) * length_scale, 0.0
    ).astype(jnp.bfloat16)
    query_grad = jnp.einsum("hqk,khd->qhd", score_grad, keys_in, preferred_element_type=jnp.float32)
    allowed = (positions[None, :] <= remote_pos[:, None]) & (positions < length)[None, :]
    scores = (
        jnp.einsum("qhd,khd->hqk", queries_in, key_heads, preferred_element_type=jnp.float32)
        * score_scale
    )
    point_weights = jnp.where(allowed[None], jax.nn.silu(scores) * length_scale, 0.0).astype(
        jnp.bfloat16
    )
    value_grad = jnp.einsum(
        "hqk,qhd->khd", point_weights, attended_in, preferred_element_type=jnp.float32
    )
    weight_grad = jnp.einsum(
        "qhd,khd->hqk", attended_in, value_heads, preferred_element_type=jnp.float32
    )
    score_grad = jnp.where(
        allowed[None], weight_grad * silu_slope(scores) * length_scale, 0.0
    ).astype(jnp.bfloat16)
    key_grad = jnp.einsum(
        "hqk,qhd->khd", score_grad, queries_in, preferred_element_type=jnp.float32
    )
    query_grad, key_grad, value_grad = (query_grad, key_grad, value_grad)
    query_grad = query_grad * score_scale
    key_grad = key_grad * score_scale
    activation_grad = jnp.concatenate(
        [
            update_grad,
            value_grad.reshape(seq_rows, hidden),
            query_grad.reshape(seq_rows, hidden),
            key_grad.reshape(seq_rows, hidden),
        ],
        axis=-1,
    )
    preact_grad = (activation_grad * silu_slope(preact)).astype(jnp.bfloat16)
    entry_grad = jnp.dot(preact_grad, input_weight.T, preferred_element_type=jnp.float32)
    features_back = jax.vjp(layer_norm, features)[1]
    input_grad = cotangent.astype(jnp.float32) + features_back(entry_grad)[0]
    back = lax.all_to_all(
        input_grad.astype(jnp.bfloat16).T.reshape(user_count, feat_cols, seq_rows),
        "col",
        split_axis=0,
        concat_axis=0,
        tiled=True,
    )
    every_grad = lax.all_gather(back, "seq", axis=0, tiled=True)
    owned_rows = item_table.shape[1] // lax.axis_size("seq")
    table_gradient = scatter(every_item, every_grad, owned_rows, seq_index)
    return (layer_output[None], table_gradient)


def solution(mesh):
    in_specs = (P(None, "seq"), P(), P("col", None), P(), P(), P("col", "seq", None))
    out_specs = (P("col", "seq", None), P("col", "seq"))
    return jax.shard_map(
        per_device, mesh=mesh, in_specs=in_specs, out_specs=out_specs, check_vma=False
    )
```

```python
import jax
import jax.numpy as jnp
from jax import lax
from jax.experimental import pallas as pl
from jax.experimental.pallas import tpu as pltpu
from jax.sharding import PartitionSpec as P

H = 8
DH = 64
LEN = 1024


norm_epsilon = 1e-05


LANES = 128
COPIES = 8
VMEM_BYTES = 58 * 1024 * 1024


def packed_place(items, feat):
    groups = LANES // feat
    row = (items // (LANES * groups)) * LANES + items % LANES
    slot = (items // LANES) % groups
    return row, slot


def lookup_kernel(rows_ref, slot_ref, table_ref, out_ref, packed, picked):
    feat, table_cols = table_ref.shape
    users, _, seq_rows = slot_ref.shape
    groups = LANES // feat
    span = LANES * groups

    def pack(block, carry):
        base = pl.multiple_of(block * span, span)
        parts = [table_ref[:, pl.ds(base + g * LANES, LANES)] for g in range(groups)]
        turned = jnp.concatenate(parts, axis=0).T
        packed[pl.ds(pl.multiple_of(block * LANES, LANES), LANES), :] = turned
        return carry

    lax.fori_loop(0, table_cols // span, pack, 0, unroll=2)

    def one_user(user, carry):
        def pick(step, inner):
            base = pl.multiple_of(step * 32, 32)
            for offset in range(32):
                row = rows_ref[user, base + offset]
                picked[pl.ds(base + offset, 1), :] = packed[pl.ds(row, 1), :]
            return inner

        lax.fori_loop(0, seq_rows // 32, pick, 0)
        for part in range(seq_rows // LANES):
            turned = picked[pl.ds(part * LANES, LANES), :].T
            slot = slot_ref[user, :, pl.ds(part * LANES, LANES)]
            total = jnp.zeros((feat, LANES), jnp.float32)
            for g in range(groups):
                total = jnp.where(slot == g, turned[g * feat : (g + 1) * feat, :], total)
            out_ref[user, :, pl.ds(part * LANES, LANES)] = total.astype(out_ref.dtype)
        return carry

    lax.fori_loop(0, users, one_user, 0)


def lookup(items, item_table):
    feat, table_cols = item_table.shape
    users, seq_rows = items.shape
    row, slot = packed_place(items, feat)
    return pl.pallas_call(
        lookup_kernel,
        out_shape=jax.ShapeDtypeStruct((users, feat, seq_rows), jnp.bfloat16),
        in_specs=[
            pl.BlockSpec(memory_space=pltpu.SMEM),
            pl.BlockSpec(memory_space=pltpu.VMEM),
            pl.BlockSpec(memory_space=pltpu.VMEM),
        ],
        out_specs=pl.BlockSpec(memory_space=pltpu.VMEM),
        scratch_shapes=[
            pltpu.VMEM((table_cols * feat // LANES, LANES), jnp.float32),
            pltpu.VMEM((seq_rows, LANES), jnp.float32),
        ],
        compiler_params=pltpu.CompilerParams(vmem_limit_bytes=VMEM_BYTES),
        name="lookup",
    )(row, slot[:, None], item_table)


def scatter_kernel(rows_ref, slot_ref, grad_ref, out_ref, placed, *sums):
    feat, owned = out_ref.shape
    blocks, _, seq_rows = slot_ref.shape
    groups = LANES // feat
    span = LANES * groups

    def clear(step, carry):
        at = pl.ds(pl.multiple_of(step * LANES, LANES), LANES)
        for total in sums:
            total[at, :] = jnp.zeros((LANES, LANES), jnp.float32)
        return carry

    lax.fori_loop(0, owned // span, clear, 0)

    def one_block(block, carry):
        for part in range(seq_rows // LANES):
            grad = grad_ref[block, :, pl.ds(part * LANES, LANES)].astype(jnp.float32)
            slot = slot_ref[block, :, pl.ds(part * LANES, LANES)]
            spread = jnp.concatenate(
                [jnp.where(slot == g, grad, 0.0) for g in range(groups)], axis=0
            )
            placed[pl.ds(part * LANES, LANES), :] = spread.T

        def add(step, inner):
            base = pl.multiple_of(step * 4 * COPIES, 4 * COPIES)
            for quarter in range(4):
                first = base + quarter * COPIES
                rows = [rows_ref[block, first + n] for n in range(COPIES)]
                news = [
                    sums[n][pl.ds(rows[n], 1), :] + placed[pl.ds(first + n, 1), :]
                    for n in range(COPIES)
                ]
                for n in range(COPIES):
                    sums[n][pl.ds(rows[n], 1), :] = news[n]
            return inner

        lax.fori_loop(0, seq_rows // (4 * COPIES), add, 0)
        return carry

    lax.fori_loop(0, blocks, one_block, 0)

    def unpack(step, carry):
        at = pl.ds(pl.multiple_of(step * LANES, LANES), LANES)
        total = sums[0][at, :]
        for other in sums[1:]:
            total = total + other[at, :]
        turned = total.T
        base = pl.multiple_of(step * span, span)
        for g in range(groups):
            out_ref[:, pl.ds(base + g * LANES, LANES)] = turned[g * feat : (g + 1) * feat, :]
        return carry

    lax.fori_loop(0, owned // span, unpack, 0, unroll=2)


def scatter(items, grads, owned, seq_index):
    feat = grads.shape[1]
    local = items % owned
    row, slot = packed_place(local, feat)
    slot = jnp.where(items // owned == seq_index, slot, -1)
    packed_rows = owned * feat // LANES
    return pl.pallas_call(
        scatter_kernel,
        out_shape=jax.ShapeDtypeStruct((feat, owned), jnp.float32),
        in_specs=[
            pl.BlockSpec(memory_space=pltpu.SMEM),
            pl.BlockSpec(memory_space=pltpu.VMEM),
            pl.BlockSpec(memory_space=pltpu.VMEM),
        ],
        out_specs=pl.BlockSpec(memory_space=pltpu.VMEM),
        scratch_shapes=[pltpu.VMEM((grads.shape[2], LANES), jnp.float32)]
        + [pltpu.VMEM((packed_rows, LANES), jnp.float32)] * COPIES,
        compiler_params=pltpu.CompilerParams(vmem_limit_bytes=VMEM_BYTES),
        name="scatter",
    )(row, slot[:, None], grads)


BLOCK = 256
F32 = jnp.float32
BF16 = jnp.bfloat16


def dot(left, right):
    return jnp.dot(left, right, preferred_element_type=F32)


def dot_last(left, right):
    return lax.dot_general(left, right, (((1,), (1,)), ((), ())), preferred_element_type=F32)


def turn(block):
    return block.astype(F32).T


def column_stats(block):
    average = jnp.mean(block, axis=0, keepdims=True)
    centered = block - average
    variance = jnp.mean(centered * centered, axis=0, keepdims=True)
    return centered, lax.rsqrt(variance + norm_epsilon)


def norm_back(normed, scale, grad):
    along = jnp.mean(grad * normed, axis=0, keepdims=True)
    return scale * (grad - jnp.mean(grad, axis=0, keepdims=True) - normed * along)


def sigmoid(block):
    return 0.5 + 0.5 * jnp.tanh(0.5 * block)


def layer_kernel(
    place_ref, own_ref, peer_ref, in_turned_ref, in_ref, out_turned_ref, out_w_ref, cot_ref,
    out_ref, entry_ref, partial_ref,
    normed, act, slope, act_peer, slope_peer, query_rows, att, scale, gated, grad_cols, grad_rows,
    point, bend, point_peer, bend_peer, pre_grad, pre_grad_peer, query_grad,
):
    hidden, rows = own_ref.shape
    seq_index = place_ref[0]
    length = place_ref[1]
    first = seq_index * rows
    score_scale = DH ** (-0.5)
    length_scale = 1.0 / LEN
    lane_pos = lax.broadcasted_iota(jnp.int32, (1, rows), 1)
    valid = lane_pos + first < length
    valid_peer = lane_pos < length
    has_peer = seq_index == 1

    def normalize(ref):
        def chunk(step, carry):
            at = pl.ds(pl.multiple_of(step * LANES, LANES), LANES)
            centered, inverse = column_stats(ref[:, at].astype(F32))
            normed[:, at] = (centered * inverse).astype(BF16)
            return carry

        lax.fori_loop(0, rows // LANES, chunk, 0)

    def project(from_row, to_row, count, act_out, slope_out, keep):
        def tile(step, carry):
            source = pl.ds(pl.multiple_of(from_row + step * BLOCK, BLOCK), BLOCK)
            target = pl.ds(pl.multiple_of(to_row + step * BLOCK, BLOCK), BLOCK)
            pre = dot(in_turned_ref[source, :], normed[...])
            sig = sigmoid(pre)
            result = pre * sig
            if keep is not None:
                result = jnp.where(keep, result, 0.0)
            act_out[target, :] = result.astype(BF16)
            slope_out[target, :] = sig * (1.0 + pre * (1.0 - sig))
            return carry

        lax.fori_loop(0, count // BLOCK, tile, 0)

    normalize(own_ref)
    project(0, 0, hidden, act, slope, None)
    project(hidden, hidden, hidden, act, slope, valid)
    project(2 * hidden, 2 * hidden, 2 * hidden, act, slope, None)

    @pl.when(has_peer)
    def _():
        normalize(peer_ref)
        project(hidden, 0, hidden, act_peer, slope_peer, valid_peer)
        project(3 * hidden, hidden, hidden, act_peer, slope_peer, None)

    def head_rows(start, head):
        return pl.ds(pl.multiple_of(start + head * DH, DH), DH)

    def weigh(scores):
        scaled = scores * score_scale
        sig = sigmoid(scaled)
        silu = scaled * sig
        return silu * length_scale, (sig + silu * (1.0 - sig)) * length_scale

    below = lax.broadcasted_iota(jnp.int32, (BLOCK, BLOCK), 1) <= lax.broadcasted_iota(
        jnp.int32, (BLOCK, BLOCK), 0
    )
    blocks = rows // BLOCK

    def forward(head, carry):
        query_rows[head] = turn(act[head_rows(2 * hidden, head), :]).astype(BF16)
        for i in range(blocks):
            at_i = pl.ds(i * BLOCK, BLOCK)
            query = query_rows[head, at_i, :]
            total = jnp.zeros((DH, BLOCK), F32)
            for j in range(i + 1):
                at_j = pl.ds(j * BLOCK, BLOCK)
                weight, curve = weigh(dot(query, act[head_rows(3 * hidden, head), at_j]))
                if i == j:
                    weight = jnp.where(below, weight, 0.0)
                    curve = jnp.where(below, curve, 0.0)
                weight = weight.astype(BF16)
                point[head, at_i, at_j] = weight
                bend[head, at_i, at_j] = curve.astype(BF16)
                total += dot_last(act[head_rows(hidden, head), at_j], weight)
            att[head_rows(0, head), at_i] = total

        @pl.when(has_peer)
        def _():
            for i in range(blocks):
                at_i = pl.ds(i * BLOCK, BLOCK)
                query = query_rows[head, at_i, :]
                weight, curve = weigh(dot(query, act_peer[head_rows(hidden, head), :]))
                weight = weight.astype(BF16)
                point_peer[head, at_i, :] = weight
                bend_peer[head, at_i, :] = curve.astype(BF16)
                att[head_rows(0, head), at_i] += dot_last(act_peer[head_rows(0, head), :], weight)

        return carry

    lax.fori_loop(0, H, forward, 0)

    def gate(step, carry):
        at = pl.ds(pl.multiple_of(step * LANES, LANES), LANES)
        centered, inverse = column_stats(att[:, at])
        normed_att = centered * inverse
        att[:, at] = normed_att
        scale[:, at] = inverse
        gated[:, at] = (normed_att * act[0:hidden, at].astype(F32)).astype(BF16)
        return carry

    lax.fori_loop(0, rows // LANES, gate, 0)

    def mix(step, carry):
        at = pl.ds(pl.multiple_of(step * LANES, LANES), LANES)
        mixed = dot(out_turned_ref[...], gated[:, at]) + own_ref[:, at].astype(F32)
        base = first + step * LANES
        row_valid = lax.broadcasted_iota(jnp.int32, (LANES, hidden), 0) + base < length
        out_ref[at, :] = jnp.where(row_valid, mixed.T, 0.0).astype(BF16)
        cot = jnp.where(row_valid, cot_ref[at, :].astype(F32), 0.0).astype(BF16)
        gated_grad = dot_last(out_w_ref[...], cot)
        normed_att = att[:, at]
        pre_grad[0:hidden, at] = (gated_grad * normed_att * slope[0:hidden, at]).astype(BF16)
        normed_grad = gated_grad * act[0:hidden, at].astype(F32)
        att_grad = norm_back(normed_att, scale[:, at], normed_grad)
        grad_cols[:, at] = att_grad.astype(BF16)
        return carry

    lax.fori_loop(0, rows // LANES, mix, 0)

    def backward(head, carry):
        grad_rows[...] = turn(grad_cols[head_rows(0, head), :]).astype(BF16)
        query_grad[...] = jnp.zeros_like(query_grad)

        @pl.when(has_peer)
        def _():
            value_total = jnp.zeros((DH, rows), F32)
            key_total = jnp.zeros((DH, rows), F32)
            for i in range(blocks):
                at_i = pl.ds(i * BLOCK, BLOCK)
                weight_grad = dot(grad_rows[at_i, :], act_peer[head_rows(0, head), :])
                score_grad = (weight_grad * bend_peer[head, at_i, :].astype(F32)).astype(BF16)
                value_total += dot(grad_cols[head_rows(0, head), at_i], point_peer[head, at_i, :])
                key_total += dot(act[head_rows(2 * hidden, head), at_i], score_grad)
                query_grad[:, at_i] = dot_last(act_peer[head_rows(hidden, head), :], score_grad)
            value_total = jnp.where(valid_peer, value_total, 0.0)
            pre_grad_peer[head_rows(0, head), :] = (
                value_total * slope_peer[head_rows(0, head), :]
            ).astype(BF16)
            pre_grad_peer[head_rows(hidden, head), :] = (
                key_total * score_scale * slope_peer[head_rows(hidden, head), :]
            ).astype(BF16)

        value_parts = [jnp.zeros((DH, BLOCK), F32) for _ in range(blocks)]
        key_parts = [jnp.zeros((DH, BLOCK), F32) for _ in range(blocks)]
        for i in range(blocks):
            at_i = pl.ds(i * BLOCK, BLOCK)
            for j in range(i + 1):
                at_j = pl.ds(j * BLOCK, BLOCK)
                weight_grad = dot(grad_rows[at_i, :], act[head_rows(hidden, head), at_j])
                score_grad = (weight_grad * bend[head, at_i, at_j].astype(F32)).astype(BF16)
                value_parts[j] += dot(grad_cols[head_rows(0, head), at_i], point[head, at_i, at_j])
                key_parts[j] += dot(act[head_rows(2 * hidden, head), at_i], score_grad)
                query_grad[:, at_i] += dot_last(act[head_rows(3 * hidden, head), at_j], score_grad)
        value_total = jnp.where(valid, jnp.concatenate(value_parts, axis=1), 0.0)
        key_total = jnp.concatenate(key_parts, axis=1) * score_scale
        for start, total in (
            (hidden, value_total),
            (2 * hidden, query_grad[...] * score_scale),
            (3 * hidden, key_total),
        ):
            at = head_rows(start, head)
            pre_grad[at, :] = (total * slope[at, :]).astype(BF16)
        return carry

    lax.fori_loop(0, H, backward, 0)

    def leave(step, carry):
        at = pl.ds(pl.multiple_of(step * BLOCK, BLOCK), BLOCK)
        entry_ref[at, :] = dot(in_ref[at, :], pre_grad[...])
        return carry

    lax.fori_loop(0, hidden // BLOCK, leave, 0)

    @pl.when(has_peer)
    def _():
        def leave_peer(step, carry):
            at = pl.ds(pl.multiple_of(step * BLOCK, BLOCK), BLOCK)
            total = dot(in_ref[at, hidden : 2 * hidden], pre_grad_peer[0:hidden, :])
            total += dot(in_ref[at, 3 * hidden :], pre_grad_peer[hidden:, :])
            partial_ref[at, :] = total.astype(BF16)
            return carry

        lax.fori_loop(0, hidden // BLOCK, leave_peer, 0)

    @pl.when(jnp.logical_not(has_peer))
    def _():
        partial_ref[...] = jnp.zeros_like(partial_ref)


def layer(place, own, peer, input_weight, output_weight, cot):
    hidden, rows = own.shape
    vmem = pl.BlockSpec(memory_space=pltpu.VMEM)
    return pl.pallas_call(
        layer_kernel,
        out_shape=(
            jax.ShapeDtypeStruct((rows, hidden), BF16),
            jax.ShapeDtypeStruct((hidden, rows), F32),
            jax.ShapeDtypeStruct((hidden, rows), BF16),
        ),
        in_specs=[pl.BlockSpec(memory_space=pltpu.SMEM)] + [vmem] * 7,
        out_specs=(vmem,) * 3,
        scratch_shapes=[
            pltpu.VMEM((hidden, rows), BF16),
            pltpu.VMEM((4 * hidden, rows), BF16),
            pltpu.VMEM((4 * hidden, rows), F32),
            pltpu.VMEM((2 * hidden, rows), BF16),
            pltpu.VMEM((2 * hidden, rows), F32),
            pltpu.VMEM((H, rows, DH), BF16),
            pltpu.VMEM((hidden, rows), F32),
            pltpu.VMEM((1, rows), F32),
            pltpu.VMEM((hidden, rows), BF16),
            pltpu.VMEM((hidden, rows), BF16),
            pltpu.VMEM((rows, DH), BF16),
            pltpu.VMEM((H, rows, rows), BF16),
            pltpu.VMEM((H, rows, rows), BF16),
            pltpu.VMEM((H, rows, rows), BF16),
            pltpu.VMEM((H, rows, rows), BF16),
            pltpu.VMEM((4 * hidden, rows), BF16),
            pltpu.VMEM((2 * hidden, rows), BF16),
            pltpu.VMEM((DH, rows), F32),
        ],
        compiler_params=pltpu.CompilerParams(vmem_limit_bytes=VMEM_BYTES),
        name="layer",
    )(place, own, peer, input_weight.T, input_weight, output_weight.T, output_weight, cot)


def finish_kernel(place_ref, own_ref, entry_ref, extra_ref, cot_ref, out_ref):
    hidden, rows = own_ref.shape
    first = place_ref[0] * rows
    length = place_ref[1]

    def chunk(step, carry):
        at = pl.ds(pl.multiple_of(step * LANES, LANES), LANES)
        centered, inverse = column_stats(own_ref[:, at].astype(F32))
        grad = entry_ref[:, at] + extra_ref[:, at].astype(F32)
        back = norm_back(centered * inverse, inverse, grad)
        lane_valid = (
            lax.broadcasted_iota(jnp.int32, (1, LANES), 1) + first + step * LANES < length
        )
        cot = jnp.where(lane_valid, turn(cot_ref[at, :]), 0.0)
        out_ref[:, at] = (cot + back).astype(BF16)
        return carry

    lax.fori_loop(0, rows // LANES, chunk, 0)


def finish(place, own, entry, extra, cot):
    vmem = pl.BlockSpec(memory_space=pltpu.VMEM)
    return pl.pallas_call(
        finish_kernel,
        out_shape=jax.ShapeDtypeStruct(own.shape, BF16),
        in_specs=[pl.BlockSpec(memory_space=pltpu.SMEM)] + [vmem] * 4,
        out_specs=vmem,
        compiler_params=pltpu.CompilerParams(vmem_limit_bytes=VMEM_BYTES),
        name="finish",
    )(place, own, entry, extra, cot)


def per_device(history_items, lengths, item_table, input_weight, output_weight, output_cotangent):
    user_count, seq_rows = history_items.shape
    feat_cols = item_table.shape[0]
    col_index = lax.axis_index("col")
    seq_index = lax.axis_index("seq")
    chosen = jnp.arange(lengths.shape[0], dtype=jnp.int32) == col_index
    length = jnp.sum(jnp.where(chosen, lengths, 0))
    place = jnp.stack([seq_index, length]).astype(jnp.int32)
    every_item = lax.all_gather(history_items, "seq", axis=0, tiled=True)
    looked = lookup(history_items, item_table)
    own = lax.all_to_all(looked, "col", split_axis=0, concat_axis=1, tiled=True)[0]
    peer = lax.ppermute(own, "seq", [(0, 1)])
    cot = output_cotangent[0]
    layer_output, entry, partial = layer(place, own, peer, input_weight, output_weight, cot)
    extra = lax.ppermute(partial, "seq", [(1, 0)])
    input_grad = finish(place, own, entry, extra, cot)
    back = lax.all_to_all(
        input_grad.reshape(user_count, feat_cols, seq_rows),
        "col",
        split_axis=0,
        concat_axis=0,
        tiled=True,
    )
    every_grad = lax.all_gather(back, "seq", axis=0, tiled=True)
    owned_rows = item_table.shape[1] // lax.axis_size("seq")
    table_gradient = scatter(every_item, every_grad, owned_rows, seq_index)
    return (layer_output[None], table_gradient)


def solution(mesh):
    in_specs = (P(None, "seq"), P(), P("col", None), P(), P(), P("col", "seq", None))
    out_specs = (P("col", "seq", None), P("col", "seq"))
    return jax.shard_map(
        per_device, mesh=mesh, in_specs=in_specs, out_specs=out_specs, check_vma=False
    )
```

```python
import jax
import jax.numpy as jnp
from jax import lax
from jax.experimental import pallas as pl
from jax.experimental.pallas import tpu as pltpu
from jax.sharding import PartitionSpec as P

H = 8
DH = 64
LEN = 1024


norm_epsilon = 1e-05


LANES = 128
MESH = pl.DeviceIdType.MESH
COPIES = 8
VMEM_BYTES = 58 * 1024 * 1024


def packed_place(items, feat):
    groups = LANES // feat
    row = (items // (LANES * groups)) * LANES + items % LANES
    slot = (items // LANES) % groups
    return row, slot


def lookup_kernel(
    rows_ref, slot_ref, table_ref, own_ref, peer_ref,
    packed, picked, slab, own, peer, own_sent, own_got, peer_sent, peer_got,
):
    feat, table_cols = table_ref.shape
    users, _, seq_rows = slot_ref.shape
    groups = LANES // feat
    span = LANES * groups
    col = lax.axis_index("col")
    seq = lax.axis_index("seq")
    barrier = pltpu.get_barrier_semaphore()
    halves = lax.axis_size("seq")

    def greet(other, carry):
        @pl.when(other != col * halves + seq)
        def _():
            pl.semaphore_signal(
                barrier, inc=1, device_id=(other // halves, other % halves), device_id_type=MESH
            )

        return carry

    lax.fori_loop(0, users * halves, greet, 0)

    def pack(block, carry):
        base = pl.multiple_of(block * span, span)
        parts = [table_ref[:, pl.ds(base + g * LANES, LANES)] for g in range(groups)]
        turned = jnp.concatenate(parts, axis=0).T
        packed[pl.ds(pl.multiple_of(block * LANES, LANES), LANES), :] = turned
        return carry

    lax.fori_loop(0, table_cols // span, pack, 0, unroll=2)
    pl.semaphore_wait(barrier, users * halves - 1)

    def to_own(user, sender):
        return pltpu.make_async_remote_copy(
            src_ref=slab.at[user],
            dst_ref=own.at[sender],
            send_sem=own_sent.at[user],
            recv_sem=own_got.at[sender],
            device_id=(user, seq),
            device_id_type=MESH,
        )

    def to_peer(user, sender):
        return pltpu.make_async_remote_copy(
            src_ref=slab.at[user],
            dst_ref=peer.at[sender],
            send_sem=peer_sent.at[user],
            recv_sem=peer_got.at[sender],
            device_id=(user, 1),
            device_id_type=MESH,
        )

    def one_user(step, carry):
        user = lax.rem(col + 1 + step, users)

        def pick(part, inner):
            base = pl.multiple_of(part * 32, 32)
            for offset in range(32):
                row = rows_ref[user, base + offset]
                picked[pl.ds(base + offset, 1), :] = packed[pl.ds(row, 1), :]
            return inner

        lax.fori_loop(0, seq_rows // 32, pick, 0)
        for part in range(seq_rows // LANES):
            turned = picked[pl.ds(part * LANES, LANES), :].T
            slot = slot_ref[user, :, pl.ds(part * LANES, LANES)]
            total = jnp.zeros((feat, LANES), jnp.float32)
            for g in range(groups):
                total = jnp.where(slot == g, turned[g * feat : (g + 1) * feat, :], total)
            slab[user, :, pl.ds(part * LANES, LANES)] = total.astype(slab.dtype)

        @pl.when(seq == 0)
        def _():
            to_peer(user, col).start()

        @pl.when(user != col)
        def _():
            to_own(user, col).start()

        return carry

    lax.fori_loop(0, users, one_user, 0)
    own_ref[col] = slab[col]

    def collect(step, carry):
        other = lax.rem(col + 1 + step, users)
        to_own(other, other).wait_recv()
        own_ref[other] = own[other]
        return carry

    lax.fori_loop(0, users - 1, collect, 0)

    @pl.when(seq == 1)
    def _():
        def collect_peer(other, carry):
            to_peer(other, other).wait_recv()
            return carry

        lax.fori_loop(0, users, collect_peer, 0)
        peer_ref[...] = peer[...]

    @pl.when(seq == 0)
    def _():
        peer_ref[...] = jnp.zeros_like(peer_ref)

    def sent(step, carry):
        other = lax.rem(col + 1 + step, users)
        to_own(other, col).wait_send()
        return carry

    lax.fori_loop(0, users - 1, sent, 0)

    @pl.when(seq == 0)
    def _():
        def sent_peer(other, carry):
            to_peer(other, col).wait_send()
            return carry

        lax.fori_loop(0, users, sent_peer, 0)


def lookup(items, item_table):
    feat, table_cols = item_table.shape
    users, seq_rows = items.shape
    row, slot = packed_place(items, feat)
    vmem = pl.BlockSpec(memory_space=pltpu.VMEM)
    slabs = (users, feat, seq_rows)
    return pl.pallas_call(
        lookup_kernel,
        out_shape=(jax.ShapeDtypeStruct(slabs, jnp.bfloat16),) * 2,
        in_specs=[pl.BlockSpec(memory_space=pltpu.SMEM), vmem, vmem],
        out_specs=(vmem, vmem),
        scratch_shapes=[
            pltpu.VMEM((table_cols * feat // LANES, LANES), jnp.float32),
            pltpu.VMEM((seq_rows, LANES), jnp.float32),
            pltpu.VMEM(slabs, jnp.bfloat16),
            pltpu.VMEM(slabs, jnp.bfloat16),
            pltpu.VMEM(slabs, jnp.bfloat16),
        ]
        + [pltpu.SemaphoreType.DMA((users,))] * 4,
        compiler_params=pltpu.CompilerParams(
            vmem_limit_bytes=VMEM_BYTES, collective_id=0, has_side_effects=True
        ),
        name="lookup",
    )(row, slot[:, None], item_table)


def scatter_kernel(rows_ref, count_ref, slot_ref, grad_ref, out_ref, placed, *sums):
    feat, owned = out_ref.shape
    blocks, _, seq_rows = slot_ref.shape
    groups = LANES // feat
    span = LANES * groups

    def clear(step, carry):
        at = pl.ds(pl.multiple_of(step * LANES, LANES), LANES)
        for total in sums:
            total[at, :] = jnp.zeros((LANES, LANES), jnp.float32)
        return carry

    lax.fori_loop(0, owned // span, clear, 0)

    def one_block(block, carry):
        count = count_ref[block]

        def place(part, inner):
            at = pl.ds(pl.multiple_of(part * LANES, LANES), LANES)
            grad = grad_ref[block, :, at].astype(jnp.float32)
            slot = slot_ref[block, :, at]
            spread = jnp.concatenate(
                [jnp.where(slot == g, grad, 0.0) for g in range(groups)], axis=0
            )
            placed[at, :] = spread.T
            return inner

        lax.fori_loop(0, (count + LANES - 1) // LANES, place, 0)

        def add(step, inner):
            base = pl.multiple_of(step * 4 * COPIES, 4 * COPIES)
            for quarter in range(4):
                first = base + quarter * COPIES
                rows = [rows_ref[block, first + n] for n in range(COPIES)]
                news = [
                    sums[n][pl.ds(rows[n], 1), :] + placed[pl.ds(first + n, 1), :]
                    for n in range(COPIES)
                ]
                for n in range(COPIES):
                    sums[n][pl.ds(rows[n], 1), :] = news[n]
            return inner

        lax.fori_loop(0, (count + 4 * COPIES - 1) // (4 * COPIES), add, 0)
        return carry

    lax.fori_loop(0, blocks, one_block, 0)

    def unpack(step, carry):
        at = pl.ds(pl.multiple_of(step * LANES, LANES), LANES)
        total = sums[0][at, :]
        for other in sums[1:]:
            total = total + other[at, :]
        turned = total.T
        base = pl.multiple_of(step * span, span)
        for g in range(groups):
            out_ref[:, pl.ds(base + g * LANES, LANES)] = turned[g * feat : (g + 1) * feat, :]
        return carry

    lax.fori_loop(0, owned // span, unpack, 0, unroll=2)


def scatter(items, counts, grads, owned, seq_index):
    feat = grads.shape[1]
    local = items % owned
    row, slot = packed_place(local, feat)
    slot = jnp.where(items // owned == seq_index, slot, -1)
    packed_rows = owned * feat // LANES
    return pl.pallas_call(
        scatter_kernel,
        out_shape=jax.ShapeDtypeStruct((feat, owned), jnp.float32),
        in_specs=[
            pl.BlockSpec(memory_space=pltpu.SMEM),
            pl.BlockSpec(memory_space=pltpu.SMEM),
            pl.BlockSpec(memory_space=pltpu.VMEM),
            pl.BlockSpec(memory_space=pltpu.VMEM),
        ],
        out_specs=pl.BlockSpec(memory_space=pltpu.VMEM),
        scratch_shapes=[pltpu.VMEM((grads.shape[2], LANES), jnp.float32)]
        + [pltpu.VMEM((packed_rows, LANES), jnp.float32)] * COPIES,
        compiler_params=pltpu.CompilerParams(vmem_limit_bytes=VMEM_BYTES),
        name="scatter",
    )(row, counts, slot[:, None], grads)


BLOCK = 256
F32 = jnp.float32
BF16 = jnp.bfloat16


def dot(left, right):
    return jnp.dot(left, right, preferred_element_type=F32)


def dot_last(left, right):
    return lax.dot_general(left, right, (((1,), (1,)), ((), ())), preferred_element_type=F32)


def turn(block):
    return block.astype(F32).T


def column_stats(block):
    average = jnp.mean(block, axis=0, keepdims=True)
    centered = block - average
    variance = jnp.mean(centered * centered, axis=0, keepdims=True)
    return centered, lax.rsqrt(variance + norm_epsilon)


def norm_back(normed, scale, grad):
    along = jnp.mean(grad * normed, axis=0, keepdims=True)
    return scale * (grad - jnp.mean(grad, axis=0, keepdims=True) - normed * along)


def sigmoid(block):
    return 0.5 + 0.5 * jnp.tanh(0.5 * block)


def layer_kernel(
    place_ref, own_ref, peer_ref, in_turned_ref, in_ref, out_turned_ref, out_w_ref, cot_ref,
    out_ref, entry_ref, partial_ref,
    normed, act, slope, act_peer, slope_peer, query_rows, att, scale, gated, grad_cols, grad_rows,
    point, bend, point_peer, bend_peer, pre_grad, pre_grad_peer, query_grad,
):
    hidden, rows = own_ref.shape
    seq_index = place_ref[0]
    length = place_ref[1]
    first = seq_index * rows
    score_scale = DH ** (-0.5)
    length_scale = 1.0 / LEN
    lane_pos = lax.broadcasted_iota(jnp.int32, (1, rows), 1)
    valid = lane_pos + first < length
    valid_peer = lane_pos < length
    has_peer = seq_index == 1

    def normalize(ref):
        def chunk(step, carry):
            at = pl.ds(pl.multiple_of(step * LANES, LANES), LANES)
            centered, inverse = column_stats(ref[:, at].astype(F32))
            normed[:, at] = (centered * inverse).astype(BF16)
            return carry

        lax.fori_loop(0, rows // LANES, chunk, 0)

    def project(from_row, to_row, count, act_out, slope_out, keep):
        def tile(step, carry):
            source = pl.ds(pl.multiple_of(from_row + step * BLOCK, BLOCK), BLOCK)
            target = pl.ds(pl.multiple_of(to_row + step * BLOCK, BLOCK), BLOCK)
            pre = dot(in_turned_ref[source, :], normed[...])
            sig = sigmoid(pre)
            result = pre * sig
            if keep is not None:
                result = jnp.where(keep, result, 0.0)
            act_out[target, :] = result.astype(BF16)
            slope_out[target, :] = sig * (1.0 + pre * (1.0 - sig))
            return carry

        lax.fori_loop(0, count // BLOCK, tile, 0)

    normalize(own_ref)
    project(0, 0, hidden, act, slope, None)
    project(hidden, hidden, hidden, act, slope, valid)
    project(2 * hidden, 2 * hidden, 2 * hidden, act, slope, None)

    @pl.when(has_peer)
    def _():
        normalize(peer_ref)
        project(hidden, 0, hidden, act_peer, slope_peer, valid_peer)
        project(3 * hidden, hidden, hidden, act_peer, slope_peer, None)

    def head_rows(start, head):
        return pl.ds(pl.multiple_of(start + head * DH, DH), DH)

    def weigh(scores):
        scaled = scores * score_scale
        sig = sigmoid(scaled)
        silu = scaled * sig
        return silu * length_scale, (sig + silu * (1.0 - sig)) * length_scale

    below = lax.broadcasted_iota(jnp.int32, (BLOCK, BLOCK), 1) <= lax.broadcasted_iota(
        jnp.int32, (BLOCK, BLOCK), 0
    )
    blocks = rows // BLOCK

    def forward(head, carry):
        query_rows[head] = turn(act[head_rows(2 * hidden, head), :]).astype(BF16)
        for i in range(blocks):
            at_i = pl.ds(i * BLOCK, BLOCK)
            query = query_rows[head, at_i, :]
            total = jnp.zeros((DH, BLOCK), F32)
            for j in range(i + 1):
                at_j = pl.ds(j * BLOCK, BLOCK)
                weight, curve = weigh(dot(query, act[head_rows(3 * hidden, head), at_j]))
                if i == j:
                    weight = jnp.where(below, weight, 0.0)
                    curve = jnp.where(below, curve, 0.0)
                weight = weight.astype(BF16)
                point[head, at_i, at_j] = weight
                bend[head, at_i, at_j] = curve.astype(BF16)
                total += dot_last(act[head_rows(hidden, head), at_j], weight)
            att[head_rows(0, head), at_i] = total

        @pl.when(has_peer)
        def _():
            for i in range(blocks):
                at_i = pl.ds(i * BLOCK, BLOCK)
                query = query_rows[head, at_i, :]
                weight, curve = weigh(dot(query, act_peer[head_rows(hidden, head), :]))
                weight = weight.astype(BF16)
                point_peer[head, at_i, :] = weight
                bend_peer[head, at_i, :] = curve.astype(BF16)
                att[head_rows(0, head), at_i] += dot_last(act_peer[head_rows(0, head), :], weight)

        return carry

    lax.fori_loop(0, H, forward, 0)

    def gate(step, carry):
        at = pl.ds(pl.multiple_of(step * LANES, LANES), LANES)
        centered, inverse = column_stats(att[:, at])
        normed_att = centered * inverse
        att[:, at] = normed_att
        scale[:, at] = inverse
        gated[:, at] = (normed_att * act[0:hidden, at].astype(F32)).astype(BF16)
        return carry

    lax.fori_loop(0, rows // LANES, gate, 0)

    def mix(step, carry):
        at = pl.ds(pl.multiple_of(step * LANES, LANES), LANES)
        mixed = dot(out_turned_ref[...], gated[:, at]) + own_ref[:, at].astype(F32)
        base = first + step * LANES
        row_valid = lax.broadcasted_iota(jnp.int32, (LANES, hidden), 0) + base < length
        out_ref[at, :] = jnp.where(row_valid, mixed.T, 0.0).astype(BF16)
        cot = jnp.where(row_valid, cot_ref[at, :].astype(F32), 0.0).astype(BF16)
        gated_grad = dot_last(out_w_ref[...], cot)
        normed_att = att[:, at]
        pre_grad[0:hidden, at] = (gated_grad * normed_att * slope[0:hidden, at]).astype(BF16)
        normed_grad = gated_grad * act[0:hidden, at].astype(F32)
        att_grad = norm_back(normed_att, scale[:, at], normed_grad)
        grad_cols[:, at] = att_grad.astype(BF16)
        return carry

    lax.fori_loop(0, rows // LANES, mix, 0)

    def backward(head, carry):
        grad_rows[...] = turn(grad_cols[head_rows(0, head), :]).astype(BF16)
        query_grad[...] = jnp.zeros_like(query_grad)

        @pl.when(has_peer)
        def _():
            value_total = jnp.zeros((DH, rows), F32)
            key_total = jnp.zeros((DH, rows), F32)
            for i in range(blocks):
                at_i = pl.ds(i * BLOCK, BLOCK)
                weight_grad = dot(grad_rows[at_i, :], act_peer[head_rows(0, head), :])
                score_grad = (weight_grad * bend_peer[head, at_i, :].astype(F32)).astype(BF16)
                value_total += dot(grad_cols[head_rows(0, head), at_i], point_peer[head, at_i, :])
                key_total += dot(act[head_rows(2 * hidden, head), at_i], score_grad)
                query_grad[:, at_i] = dot_last(act_peer[head_rows(hidden, head), :], score_grad)
            value_total = jnp.where(valid_peer, value_total, 0.0)
            pre_grad_peer[head_rows(0, head), :] = (
                value_total * slope_peer[head_rows(0, head), :]
            ).astype(BF16)
            pre_grad_peer[head_rows(hidden, head), :] = (
                key_total * score_scale * slope_peer[head_rows(hidden, head), :]
            ).astype(BF16)

        value_parts = [jnp.zeros((DH, BLOCK), F32) for _ in range(blocks)]
        key_parts = [jnp.zeros((DH, BLOCK), F32) for _ in range(blocks)]
        for i in range(blocks):
            at_i = pl.ds(i * BLOCK, BLOCK)
            for j in range(i + 1):
                at_j = pl.ds(j * BLOCK, BLOCK)
                weight_grad = dot(grad_rows[at_i, :], act[head_rows(hidden, head), at_j])
                score_grad = (weight_grad * bend[head, at_i, at_j].astype(F32)).astype(BF16)
                value_parts[j] += dot(grad_cols[head_rows(0, head), at_i], point[head, at_i, at_j])
                key_parts[j] += dot(act[head_rows(2 * hidden, head), at_i], score_grad)
                query_grad[:, at_i] += dot_last(act[head_rows(3 * hidden, head), at_j], score_grad)
        value_total = jnp.where(valid, jnp.concatenate(value_parts, axis=1), 0.0)
        key_total = jnp.concatenate(key_parts, axis=1) * score_scale
        for start, total in (
            (hidden, value_total),
            (2 * hidden, query_grad[...] * score_scale),
            (3 * hidden, key_total),
        ):
            at = head_rows(start, head)
            pre_grad[at, :] = (total * slope[at, :]).astype(BF16)
        return carry

    lax.fori_loop(0, H, backward, 0)

    def leave(step, carry):
        at = pl.ds(pl.multiple_of(step * BLOCK, BLOCK), BLOCK)
        entry_ref[at, :] = dot(in_ref[at, :], pre_grad[...])
        return carry

    lax.fori_loop(0, hidden // BLOCK, leave, 0)

    @pl.when(has_peer)
    def _():
        def leave_peer(step, carry):
            at = pl.ds(pl.multiple_of(step * BLOCK, BLOCK), BLOCK)
            total = dot(in_ref[at, hidden : 2 * hidden], pre_grad_peer[0:hidden, :])
            total += dot(in_ref[at, 3 * hidden :], pre_grad_peer[hidden:, :])
            partial_ref[at, :] = total.astype(BF16)
            return carry

        lax.fori_loop(0, hidden // BLOCK, leave_peer, 0)

    @pl.when(jnp.logical_not(has_peer))
    def _():
        partial_ref[...] = jnp.zeros_like(partial_ref)


def layer(place, own, peer, input_weight, output_weight, cot):
    hidden, rows = own.shape
    vmem = pl.BlockSpec(memory_space=pltpu.VMEM)
    return pl.pallas_call(
        layer_kernel,
        out_shape=(
            jax.ShapeDtypeStruct((rows, hidden), BF16),
            jax.ShapeDtypeStruct((hidden, rows), F32),
            jax.ShapeDtypeStruct((hidden, rows), BF16),
        ),
        in_specs=[pl.BlockSpec(memory_space=pltpu.SMEM)] + [vmem] * 7,
        out_specs=(vmem,) * 3,
        scratch_shapes=[
            pltpu.VMEM((hidden, rows), BF16),
            pltpu.VMEM((4 * hidden, rows), BF16),
            pltpu.VMEM((4 * hidden, rows), F32),
            pltpu.VMEM((2 * hidden, rows), BF16),
            pltpu.VMEM((2 * hidden, rows), F32),
            pltpu.VMEM((H, rows, DH), BF16),
            pltpu.VMEM((hidden, rows), F32),
            pltpu.VMEM((1, rows), F32),
            pltpu.VMEM((hidden, rows), BF16),
            pltpu.VMEM((hidden, rows), BF16),
            pltpu.VMEM((rows, DH), BF16),
            pltpu.VMEM((H, rows, rows), BF16),
            pltpu.VMEM((H, rows, rows), BF16),
            pltpu.VMEM((H, rows, rows), BF16),
            pltpu.VMEM((H, rows, rows), BF16),
            pltpu.VMEM((4 * hidden, rows), BF16),
            pltpu.VMEM((2 * hidden, rows), BF16),
            pltpu.VMEM((DH, rows), F32),
        ],
        compiler_params=pltpu.CompilerParams(vmem_limit_bytes=VMEM_BYTES),
        name="layer",
    )(place, own, peer, input_weight.T, input_weight, output_weight.T, output_weight, cot)


def finish_kernel(place_ref, own_ref, entry_ref, extra_ref, cot_ref, out_ref):
    hidden, rows = own_ref.shape
    first = place_ref[0] * rows
    length = place_ref[1]

    def chunk(step, carry):
        at = pl.ds(pl.multiple_of(step * LANES, LANES), LANES)
        centered, inverse = column_stats(own_ref[:, at].astype(F32))
        grad = entry_ref[:, at] + extra_ref[:, at].astype(F32)
        back = norm_back(centered * inverse, inverse, grad)
        lane_valid = (
            lax.broadcasted_iota(jnp.int32, (1, LANES), 1) + first + step * LANES < length
        )
        cot = jnp.where(lane_valid, turn(cot_ref[at, :]), 0.0)
        out_ref[:, at] = (cot + back).astype(BF16)
        return carry

    lax.fori_loop(0, rows // LANES, chunk, 0)


def finish(place, own, entry, extra, cot):
    vmem = pl.BlockSpec(memory_space=pltpu.VMEM)
    return pl.pallas_call(
        finish_kernel,
        out_shape=jax.ShapeDtypeStruct(own.shape, BF16),
        in_specs=[pl.BlockSpec(memory_space=pltpu.SMEM)] + [vmem] * 4,
        out_specs=vmem,
        compiler_params=pltpu.CompilerParams(vmem_limit_bytes=VMEM_BYTES),
        name="finish",
    )(place, own, entry, extra, cot)


def per_device(history_items, lengths, item_table, input_weight, output_weight, output_cotangent):
    user_count, seq_rows = history_items.shape
    feat_cols = item_table.shape[0]
    col_index = lax.axis_index("col")
    seq_index = lax.axis_index("seq")
    chosen = jnp.arange(lengths.shape[0], dtype=jnp.int32) == col_index
    length = jnp.sum(jnp.where(chosen, lengths, 0))
    place = jnp.stack([seq_index, length]).astype(jnp.int32)
    every_item = lax.all_gather(history_items, "seq", axis=0, tiled=True)
    own, peer = lookup(history_items, item_table)
    own = own.reshape(user_count * feat_cols, seq_rows)
    peer = peer.reshape(user_count * feat_cols, seq_rows)
    cot = output_cotangent[0]
    layer_output, entry, partial = layer(place, own, peer, input_weight, output_weight, cot)
    extra = lax.ppermute(partial, "seq", [(1, 0)])
    input_grad = finish(place, own, entry, extra, cot)
    back = lax.all_to_all(
        input_grad.reshape(user_count, feat_cols, seq_rows),
        "col",
        split_axis=0,
        concat_axis=0,
        tiled=True,
    )
    every_grad = lax.all_gather(back, "seq", axis=0, tiled=True)
    starts = seq_rows * jnp.arange(lax.axis_size("seq"), dtype=jnp.int32)
    counts = jnp.clip(lengths[None, :] - starts[:, None], 0, seq_rows).reshape(-1)
    owned_rows = item_table.shape[1] // lax.axis_size("seq")
    table_gradient = scatter(every_item, counts, every_grad, owned_rows, seq_index)
    return (layer_output[None], table_gradient)


def solution(mesh):
    in_specs = (P(None, "seq"), P(), P("col", None), P(), P(), P("col", "seq", None))
    out_specs = (P("col", "seq", None), P("col", "seq"))
    return jax.shard_map(
        per_device, mesh=mesh, in_specs=in_specs, out_specs=out_specs, check_vma=False
    )
```

```python
import jax
import jax.numpy as jnp
from jax import lax
from jax.experimental import pallas as pl
from jax.experimental.pallas import tpu as pltpu
from jax.sharding import PartitionSpec as P

H = 8
DH = 64
LEN = 1024


norm_epsilon = 1e-05


LANES = 128
MESH = pl.DeviceIdType.MESH
COPIES = 8
VMEM_BYTES = 58 * 1024 * 1024


def packed_place(items, feat):
    groups = LANES // feat
    row = (items // (LANES * groups)) * LANES + items % LANES
    slot = (items // LANES) % groups
    return row, slot


def lookup_kernel(
    rows_ref, slot_ref, table_ref, items_ref, own_ref, peer_ref, twin_items_ref,
    packed, picked, slab, own, peer, twin, own_sent, own_got, peer_sent, peer_got, twin_sems,
):
    feat, table_cols = table_ref.shape
    users, _, seq_rows = slot_ref.shape
    groups = LANES // feat
    span = LANES * groups
    col = lax.axis_index("col")
    seq = lax.axis_index("seq")
    barrier = pltpu.get_barrier_semaphore()
    halves = lax.axis_size("seq")

    greet_all(barrier, users, halves, col * halves + seq)

    def pack(block, carry):
        base = pl.multiple_of(block * span, span)
        parts = [table_ref[:, pl.ds(base + g * LANES, LANES)] for g in range(groups)]
        turned = jnp.concatenate(parts, axis=0).T
        packed[pl.ds(pl.multiple_of(block * LANES, LANES), LANES), :] = turned
        return carry

    lax.fori_loop(0, table_cols // span, pack, 0, unroll=2)
    pl.semaphore_wait(barrier, users * halves - 1)
    items_copy = pltpu.make_async_remote_copy(
        src_ref=items_ref,
        dst_ref=twin,
        send_sem=twin_sems.at[0],
        recv_sem=twin_sems.at[1],
        device_id=(col, 1 - seq),
        device_id_type=MESH,
    )
    items_copy.start()

    def to_own(user, sender):
        return pltpu.make_async_remote_copy(
            src_ref=slab.at[user],
            dst_ref=own.at[sender],
            send_sem=own_sent.at[user],
            recv_sem=own_got.at[sender],
            device_id=(user, seq),
            device_id_type=MESH,
        )

    def to_peer(user, sender):
        return pltpu.make_async_remote_copy(
            src_ref=slab.at[user],
            dst_ref=peer.at[sender],
            send_sem=peer_sent.at[user],
            recv_sem=peer_got.at[sender],
            device_id=(user, 1),
            device_id_type=MESH,
        )

    def one_user(step, carry):
        user = lax.rem(col + 1 + step, users)

        def pick(part, inner):
            base = pl.multiple_of(part * 32, 32)
            for offset in range(32):
                row = rows_ref[user, base + offset]
                picked[pl.ds(base + offset, 1), :] = packed[pl.ds(row, 1), :]
            return inner

        lax.fori_loop(0, seq_rows // 32, pick, 0)
        for part in range(seq_rows // LANES):
            turned = picked[pl.ds(part * LANES, LANES), :].T
            slot = slot_ref[user, :, pl.ds(part * LANES, LANES)]
            total = jnp.zeros((feat, LANES), jnp.float32)
            for g in range(groups):
                total = jnp.where(slot == g, turned[g * feat : (g + 1) * feat, :], total)
            slab[user, :, pl.ds(part * LANES, LANES)] = total.astype(slab.dtype)

        @pl.when(seq == 0)
        def _():
            to_peer(user, col).start()

        @pl.when(user != col)
        def _():
            to_own(user, col).start()

        return carry

    lax.fori_loop(0, users, one_user, 0)
    own_ref[col] = slab[col]
    items_copy.wait()
    twin_items_ref[...] = twin[...]

    def collect(step, carry):
        other = lax.rem(col + 1 + step, users)
        to_own(other, other).wait_recv()
        own_ref[other] = own[other]
        return carry

    lax.fori_loop(0, users - 1, collect, 0)

    @pl.when(seq == 1)
    def _():
        def collect_peer(other, carry):
            to_peer(other, other).wait_recv()
            return carry

        lax.fori_loop(0, users, collect_peer, 0)
        peer_ref[...] = peer[...]

    @pl.when(seq == 0)
    def _():
        peer_ref[...] = jnp.zeros_like(peer_ref)

    def sent(step, carry):
        other = lax.rem(col + 1 + step, users)
        to_own(other, col).wait_send()
        return carry

    lax.fori_loop(0, users - 1, sent, 0)

    @pl.when(seq == 0)
    def _():
        def sent_peer(other, carry):
            to_peer(other, col).wait_send()
            return carry

        lax.fori_loop(0, users, sent_peer, 0)


def lookup(items, item_table):
    feat, table_cols = item_table.shape
    users, seq_rows = items.shape
    row, slot = packed_place(items, feat)
    vmem = pl.BlockSpec(memory_space=pltpu.VMEM)
    slabs = (users, feat, seq_rows)
    return pl.pallas_call(
        lookup_kernel,
        out_shape=(jax.ShapeDtypeStruct(slabs, jnp.bfloat16),) * 2
        + (jax.ShapeDtypeStruct(items.shape, items.dtype),),
        in_specs=[pl.BlockSpec(memory_space=pltpu.SMEM), vmem, vmem, vmem],
        out_specs=(vmem,) * 3,
        scratch_shapes=[
            pltpu.VMEM((table_cols * feat // LANES, LANES), jnp.float32),
            pltpu.VMEM((seq_rows, LANES), jnp.float32),
            pltpu.VMEM(slabs, jnp.bfloat16),
            pltpu.VMEM(slabs, jnp.bfloat16),
            pltpu.VMEM(slabs, jnp.bfloat16),
            pltpu.VMEM(items.shape, items.dtype),
        ]
        + [pltpu.SemaphoreType.DMA((users,))] * 4
        + [pltpu.SemaphoreType.DMA((2,))],
        compiler_params=pltpu.CompilerParams(
            vmem_limit_bytes=VMEM_BYTES, collective_id=0, has_side_effects=True
        ),
        name="lookup",
    )(row, slot[:, None], item_table, items)


def scatter_kernel(rows_ref, count_ref, slot_ref, grad_ref, out_ref, placed, *sums):
    feat, owned = out_ref.shape
    blocks, _, seq_rows = slot_ref.shape
    groups = LANES // feat
    span = LANES * groups

    def clear(step, carry):
        at = pl.ds(pl.multiple_of(step * LANES, LANES), LANES)
        for total in sums:
            total[at, :] = jnp.zeros((LANES, LANES), jnp.float32)
        return carry

    lax.fori_loop(0, owned // span, clear, 0)

    def one_block(block, carry):
        count = count_ref[block]

        def place(part, inner):
            at = pl.ds(pl.multiple_of(part * LANES, LANES), LANES)
            grad = grad_ref[block, :, at].astype(jnp.float32)
            slot = slot_ref[block, :, at]
            spread = jnp.concatenate(
                [jnp.where(slot == g, grad, 0.0) for g in range(groups)], axis=0
            )
            placed[at, :] = spread.T
            return inner

        lax.fori_loop(0, (count + LANES - 1) // LANES, place, 0)

        def add(step, inner):
            base = pl.multiple_of(step * 4 * COPIES, 4 * COPIES)
            for quarter in range(4):
                first = base + quarter * COPIES
                rows = [rows_ref[block, first + n] for n in range(COPIES)]
                news = [
                    sums[n][pl.ds(rows[n], 1), :] + placed[pl.ds(first + n, 1), :]
                    for n in range(COPIES)
                ]
                for n in range(COPIES):
                    sums[n][pl.ds(rows[n], 1), :] = news[n]
            return inner

        lax.fori_loop(0, (count + 4 * COPIES - 1) // (4 * COPIES), add, 0)
        return carry

    lax.fori_loop(0, blocks, one_block, 0)

    def unpack(step, carry):
        at = pl.ds(pl.multiple_of(step * LANES, LANES), LANES)
        total = sums[0][at, :]
        for other in sums[1:]:
            total = total + other[at, :]
        turned = total.T
        base = pl.multiple_of(step * span, span)
        for g in range(groups):
            out_ref[:, pl.ds(base + g * LANES, LANES)] = turned[g * feat : (g + 1) * feat, :]
        return carry

    lax.fori_loop(0, owned // span, unpack, 0, unroll=2)


def scatter(items, counts, grads, owned, seq_index):
    feat = grads.shape[1]
    local = items % owned
    row, slot = packed_place(local, feat)
    slot = jnp.where(items // owned == seq_index, slot, -1)
    packed_rows = owned * feat // LANES
    return pl.pallas_call(
        scatter_kernel,
        out_shape=jax.ShapeDtypeStruct((feat, owned), jnp.float32),
        in_specs=[
            pl.BlockSpec(memory_space=pltpu.SMEM),
            pl.BlockSpec(memory_space=pltpu.SMEM),
            pl.BlockSpec(memory_space=pltpu.VMEM),
            pl.BlockSpec(memory_space=pltpu.VMEM),
        ],
        out_specs=pl.BlockSpec(memory_space=pltpu.VMEM),
        scratch_shapes=[pltpu.VMEM((grads.shape[2], LANES), jnp.float32)]
        + [pltpu.VMEM((packed_rows, LANES), jnp.float32)] * COPIES,
        compiler_params=pltpu.CompilerParams(vmem_limit_bytes=VMEM_BYTES),
        name="scatter",
    )(row, counts, slot[:, None], grads)


BLOCK = 256
F32 = jnp.float32
BF16 = jnp.bfloat16


def dot(left, right):
    return jnp.dot(left, right, preferred_element_type=F32)


def dot_last(left, right):
    return lax.dot_general(left, right, (((1,), (1,)), ((), ())), preferred_element_type=F32)


def turn(block):
    return block.astype(F32).T


def column_stats(block):
    average = jnp.mean(block, axis=0, keepdims=True)
    centered = block - average
    variance = jnp.mean(centered * centered, axis=0, keepdims=True)
    return centered, lax.rsqrt(variance + norm_epsilon)


def norm_back(normed, scale, grad):
    along = jnp.mean(grad * normed, axis=0, keepdims=True)
    return scale * (grad - jnp.mean(grad, axis=0, keepdims=True) - normed * along)


def sigmoid(block):
    return 0.5 + 0.5 * jnp.tanh(0.5 * block)


def layer_kernel(
    lengths_ref, own_ref, peer_ref, in_turned_ref, in_ref, out_turned_ref, out_w_ref, cot_ref,
    out_ref, entry_ref, partial_ref,
    normed, act, slope, act_peer, slope_peer, query_rows, att, scale, gated, grad_cols, grad_rows,
    point, bend, point_peer, bend_peer, pre_grad, pre_grad_peer, query_grad,
):
    hidden, rows = own_ref.shape
    seq_index = lax.axis_index("seq")
    length = lengths_ref[lax.axis_index("col")]
    first = seq_index * rows
    score_scale = DH ** (-0.5)
    length_scale = 1.0 / LEN
    lane_pos = lax.broadcasted_iota(jnp.int32, (1, rows), 1)
    valid = lane_pos + first < length
    valid_peer = lane_pos < length
    has_peer = seq_index == 1

    def normalize(ref):
        def chunk(step, carry):
            at = pl.ds(pl.multiple_of(step * LANES, LANES), LANES)
            centered, inverse = column_stats(ref[:, at].astype(F32))
            normed[:, at] = (centered * inverse).astype(BF16)
            return carry

        lax.fori_loop(0, rows // LANES, chunk, 0)

    def project(from_row, to_row, count, act_out, slope_out, keep):
        def tile(step, carry):
            source = pl.ds(pl.multiple_of(from_row + step * BLOCK, BLOCK), BLOCK)
            target = pl.ds(pl.multiple_of(to_row + step * BLOCK, BLOCK), BLOCK)
            pre = dot(in_turned_ref[source, :], normed[...])
            sig = sigmoid(pre)
            result = pre * sig
            if keep is not None:
                result = jnp.where(keep, result, 0.0)
            act_out[target, :] = result.astype(BF16)
            slope_out[target, :] = sig * (1.0 + pre * (1.0 - sig))
            return carry

        lax.fori_loop(0, count // BLOCK, tile, 0)

    normalize(own_ref)
    project(0, 0, hidden, act, slope, None)
    project(hidden, hidden, hidden, act, slope, valid)
    project(2 * hidden, 2 * hidden, 2 * hidden, act, slope, None)

    @pl.when(has_peer)
    def _():
        normalize(peer_ref)
        project(hidden, 0, hidden, act_peer, slope_peer, valid_peer)
        project(3 * hidden, hidden, hidden, act_peer, slope_peer, None)

    def head_rows(start, head):
        return pl.ds(pl.multiple_of(start + head * DH, DH), DH)

    def weigh(scores):
        scaled = scores * score_scale
        sig = sigmoid(scaled)
        silu = scaled * sig
        return silu * length_scale, (sig + silu * (1.0 - sig)) * length_scale

    below = lax.broadcasted_iota(jnp.int32, (BLOCK, BLOCK), 1) <= lax.broadcasted_iota(
        jnp.int32, (BLOCK, BLOCK), 0
    )
    blocks = rows // BLOCK

    def forward(head, carry):
        query_rows[head] = turn(act[head_rows(2 * hidden, head), :]).astype(BF16)
        for i in range(blocks):
            at_i = pl.ds(i * BLOCK, BLOCK)
            query = query_rows[head, at_i, :]
            total = jnp.zeros((DH, BLOCK), F32)
            for j in range(i + 1):
                at_j = pl.ds(j * BLOCK, BLOCK)
                weight, curve = weigh(dot(query, act[head_rows(3 * hidden, head), at_j]))
                if i == j:
                    weight = jnp.where(below, weight, 0.0)
                    curve = jnp.where(below, curve, 0.0)
                weight = weight.astype(BF16)
                point[head, at_i, at_j] = weight
                bend[head, at_i, at_j] = curve.astype(BF16)
                total += dot_last(act[head_rows(hidden, head), at_j], weight)
            att[head_rows(0, head), at_i] = total

        @pl.when(has_peer)
        def _():
            for i in range(blocks):
                at_i = pl.ds(i * BLOCK, BLOCK)
                query = query_rows[head, at_i, :]
                weight, curve = weigh(dot(query, act_peer[head_rows(hidden, head), :]))
                weight = weight.astype(BF16)
                point_peer[head, at_i, :] = weight
                bend_peer[head, at_i, :] = curve.astype(BF16)
                att[head_rows(0, head), at_i] += dot_last(act_peer[head_rows(0, head), :], weight)

        return carry

    lax.fori_loop(0, H, forward, 0)

    def gate(step, carry):
        at = pl.ds(pl.multiple_of(step * LANES, LANES), LANES)
        centered, inverse = column_stats(att[:, at])
        normed_att = centered * inverse
        att[:, at] = normed_att
        scale[:, at] = inverse
        gated[:, at] = (normed_att * act[0:hidden, at].astype(F32)).astype(BF16)
        return carry

    lax.fori_loop(0, rows // LANES, gate, 0)

    def mix(step, carry):
        at = pl.ds(pl.multiple_of(step * LANES, LANES), LANES)
        mixed = dot(out_turned_ref[...], gated[:, at]) + own_ref[:, at].astype(F32)
        base = first + step * LANES
        row_valid = lax.broadcasted_iota(jnp.int32, (LANES, hidden), 0) + base < length
        out_ref[at, :] = jnp.where(row_valid, mixed.T, 0.0).astype(BF16)
        cot = jnp.where(row_valid, cot_ref[at, :].astype(F32), 0.0).astype(BF16)
        gated_grad = dot_last(out_w_ref[...], cot)
        normed_att = att[:, at]
        pre_grad[0:hidden, at] = (gated_grad * normed_att * slope[0:hidden, at]).astype(BF16)
        normed_grad = gated_grad * act[0:hidden, at].astype(F32)
        att_grad = norm_back(normed_att, scale[:, at], normed_grad)
        grad_cols[:, at] = att_grad.astype(BF16)
        return carry

    lax.fori_loop(0, rows // LANES, mix, 0)

    def backward(head, carry):
        grad_rows[...] = turn(grad_cols[head_rows(0, head), :]).astype(BF16)
        query_grad[...] = jnp.zeros_like(query_grad)

        @pl.when(has_peer)
        def _():
            value_total = jnp.zeros((DH, rows), F32)
            key_total = jnp.zeros((DH, rows), F32)
            for i in range(blocks):
                at_i = pl.ds(i * BLOCK, BLOCK)
                weight_grad = dot(grad_rows[at_i, :], act_peer[head_rows(0, head), :])
                score_grad = (weight_grad * bend_peer[head, at_i, :].astype(F32)).astype(BF16)
                value_total += dot(grad_cols[head_rows(0, head), at_i], point_peer[head, at_i, :])
                key_total += dot(act[head_rows(2 * hidden, head), at_i], score_grad)
                query_grad[:, at_i] = dot_last(act_peer[head_rows(hidden, head), :], score_grad)
            value_total = jnp.where(valid_peer, value_total, 0.0)
            pre_grad_peer[head_rows(0, head), :] = (
                value_total * slope_peer[head_rows(0, head), :]
            ).astype(BF16)
            pre_grad_peer[head_rows(hidden, head), :] = (
                key_total * score_scale * slope_peer[head_rows(hidden, head), :]
            ).astype(BF16)

        value_parts = [jnp.zeros((DH, BLOCK), F32) for _ in range(blocks)]
        key_parts = [jnp.zeros((DH, BLOCK), F32) for _ in range(blocks)]
        for i in range(blocks):
            at_i = pl.ds(i * BLOCK, BLOCK)
            for j in range(i + 1):
                at_j = pl.ds(j * BLOCK, BLOCK)
                weight_grad = dot(grad_rows[at_i, :], act[head_rows(hidden, head), at_j])
                score_grad = (weight_grad * bend[head, at_i, at_j].astype(F32)).astype(BF16)
                value_parts[j] += dot(grad_cols[head_rows(0, head), at_i], point[head, at_i, at_j])
                key_parts[j] += dot(act[head_rows(2 * hidden, head), at_i], score_grad)
                query_grad[:, at_i] += dot_last(act[head_rows(3 * hidden, head), at_j], score_grad)
        value_total = jnp.where(valid, jnp.concatenate(value_parts, axis=1), 0.0)
        key_total = jnp.concatenate(key_parts, axis=1) * score_scale
        for start, total in (
            (hidden, value_total),
            (2 * hidden, query_grad[...] * score_scale),
            (3 * hidden, key_total),
        ):
            at = head_rows(start, head)
            pre_grad[at, :] = (total * slope[at, :]).astype(BF16)
        return carry

    lax.fori_loop(0, H, backward, 0)

    def leave(step, carry):
        at = pl.ds(pl.multiple_of(step * BLOCK, BLOCK), BLOCK)
        entry_ref[at, :] = dot(in_ref[at, :], pre_grad[...])
        return carry

    lax.fori_loop(0, hidden // BLOCK, leave, 0)

    @pl.when(has_peer)
    def _():
        def leave_peer(step, carry):
            at = pl.ds(pl.multiple_of(step * BLOCK, BLOCK), BLOCK)
            total = dot(in_ref[at, hidden : 2 * hidden], pre_grad_peer[0:hidden, :])
            total += dot(in_ref[at, 3 * hidden :], pre_grad_peer[hidden:, :])
            partial_ref[at, :] = total.astype(BF16)
            return carry

        lax.fori_loop(0, hidden // BLOCK, leave_peer, 0)

    @pl.when(jnp.logical_not(has_peer))
    def _():
        partial_ref[...] = jnp.zeros_like(partial_ref)


def layer(lengths, own, peer, input_weight, output_weight, cot):
    hidden, rows = own.shape
    vmem = pl.BlockSpec(memory_space=pltpu.VMEM)
    return pl.pallas_call(
        layer_kernel,
        out_shape=(
            jax.ShapeDtypeStruct((rows, hidden), BF16),
            jax.ShapeDtypeStruct((hidden, rows), F32),
            jax.ShapeDtypeStruct((hidden, rows), BF16),
        ),
        in_specs=[pl.BlockSpec(memory_space=pltpu.SMEM)] + [vmem] * 7,
        out_specs=(vmem,) * 3,
        scratch_shapes=[
            pltpu.VMEM((hidden, rows), BF16),
            pltpu.VMEM((4 * hidden, rows), BF16),
            pltpu.VMEM((4 * hidden, rows), F32),
            pltpu.VMEM((2 * hidden, rows), BF16),
            pltpu.VMEM((2 * hidden, rows), F32),
            pltpu.VMEM((H, rows, DH), BF16),
            pltpu.VMEM((hidden, rows), F32),
            pltpu.VMEM((1, rows), F32),
            pltpu.VMEM((hidden, rows), BF16),
            pltpu.VMEM((hidden, rows), BF16),
            pltpu.VMEM((rows, DH), BF16),
            pltpu.VMEM((H, rows, rows), BF16),
            pltpu.VMEM((H, rows, rows), BF16),
            pltpu.VMEM((H, rows, rows), BF16),
            pltpu.VMEM((H, rows, rows), BF16),
            pltpu.VMEM((4 * hidden, rows), BF16),
            pltpu.VMEM((2 * hidden, rows), BF16),
            pltpu.VMEM((DH, rows), F32),
        ],
        compiler_params=pltpu.CompilerParams(vmem_limit_bytes=VMEM_BYTES),
        name="layer",
    )(lengths, own, peer, input_weight.T, input_weight, output_weight.T, output_weight, cot)


def greet_all(barrier, users, halves, me):
    def greet(other, carry):
        @pl.when(other != me)
        def _():
            pl.semaphore_signal(
                barrier, inc=1, device_id=(other // halves, other % halves), device_id_type=MESH
            )

        return carry

    lax.fori_loop(0, users * halves, greet, 0)


def back_kernel(
    lengths_ref, own_ref, entry_ref, partial_ref, cot_ref, out_ref,
    extra, grad, mine, others, extra_sems, sent, got, passed, passed_got,
):
    hidden, rows = own_ref.shape
    users, feat, _ = grad.shape
    halves = lax.axis_size("seq")
    col = lax.axis_index("col")
    seq = lax.axis_index("seq")
    length = lengths_ref[col]
    first = seq * rows
    barrier = pltpu.get_barrier_semaphore()
    greet_all(barrier, users, halves, col * halves + seq)
    pl.semaphore_wait(barrier, users * halves - 1)

    extra_copy = pltpu.make_async_remote_copy(
        src_ref=partial_ref,
        dst_ref=extra,
        send_sem=extra_sems.at[0],
        recv_sem=extra_sems.at[1],
        device_id=(col, 0),
        device_id_type=MESH,
    )

    @pl.when(seq == 1)
    def _():
        extra_copy.start()

    def chunk(step, carry):
        at = pl.ds(pl.multiple_of(step * LANES, LANES), LANES)
        centered, inverse = column_stats(own_ref[:, at].astype(F32))
        received = jnp.where(seq == 0, extra[:, at].astype(F32), 0.0)
        back = norm_back(centered * inverse, inverse, entry_ref[:, at] + received)
        lane_valid = (
            lax.broadcasted_iota(jnp.int32, (1, LANES), 1) + first + step * LANES < length
        )
        total = jnp.where(lane_valid, turn(cot_ref[at, :]), 0.0) + back
        grad[:, :, at] = total.reshape(users, feat, LANES).astype(BF16)
        return carry

    @pl.when(seq == 1)
    def _():
        extra[...] = jnp.zeros_like(extra)

    @pl.when(seq == 0)
    def _():
        extra_copy.wait_recv()

    lax.fori_loop(0, rows // LANES, chunk, 0)

    def to_owner(user, sender):
        return pltpu.make_async_remote_copy(
            src_ref=grad.at[user],
            dst_ref=mine.at[sender],
            send_sem=sent.at[user],
            recv_sem=got.at[sender],
            device_id=(user, seq),
            device_id_type=MESH,
        )

    def to_twin(source, sender):
        return pltpu.make_async_remote_copy(
            src_ref=source.at[sender],
            dst_ref=others.at[sender],
            send_sem=passed.at[sender],
            recv_sem=passed_got.at[sender],
            device_id=(col, 1 - seq),
            device_id_type=MESH,
        )

    def send(step, carry):
        user = lax.rem(col + 1 + step, users)
        to_owner(user, col).start()
        return carry

    lax.fori_loop(0, users - 1, send, 0)
    to_twin(grad, col).start()
    out_ref[col] = grad[col]

    def forward(step, carry):
        sender = lax.rem(col + users - 1 - step, users)
        to_owner(sender, sender).wait_recv()
        to_twin(mine, sender).start()
        out_ref[sender] = mine[sender]
        return carry

    lax.fori_loop(0, users - 1, forward, 0)

    def collect(step, carry):
        sender = lax.rem(col + users - step, users)
        to_twin(mine, sender).wait_recv()
        out_ref[users + sender] = others[sender]
        return carry

    lax.fori_loop(0, users, collect, 0)

    def leave(step, carry):
        user = lax.rem(col + 1 + step, users)
        to_owner(user, col).wait_send()
        to_twin(mine, user).wait_send()
        return carry

    lax.fori_loop(0, users - 1, leave, 0)
    to_twin(grad, col).wait_send()

    @pl.when(seq == 1)
    def _():
        extra_copy.wait_send()


def send_back(lengths, own, entry, partial, cot, users):
    hidden, rows = own.shape
    vmem = pl.BlockSpec(memory_space=pltpu.VMEM)
    slabs = (users, hidden // users, rows)
    return pl.pallas_call(
        back_kernel,
        out_shape=jax.ShapeDtypeStruct((2 * users,) + slabs[1:], BF16),
        in_specs=[pl.BlockSpec(memory_space=pltpu.SMEM)] + [vmem] * 4,
        out_specs=vmem,
        scratch_shapes=[pltpu.VMEM((hidden, rows), BF16)]
        + [pltpu.VMEM(slabs, BF16)] * 3
        + [pltpu.SemaphoreType.DMA((2,))]
        + [pltpu.SemaphoreType.DMA((users,))] * 4,
        compiler_params=pltpu.CompilerParams(
            vmem_limit_bytes=VMEM_BYTES, collective_id=1, has_side_effects=True
        ),
        name="send_back",
    )(lengths, own, entry, partial, cot)


def per_device(history_items, lengths, item_table, input_weight, output_weight, output_cotangent):
    user_count, seq_rows = history_items.shape
    feat_cols = item_table.shape[0]
    seq_index = lax.axis_index("seq")
    own, peer, twin_items = lookup(history_items, item_table)
    own = own.reshape(user_count * feat_cols, seq_rows)
    peer = peer.reshape(user_count * feat_cols, seq_rows)
    cot = output_cotangent[0]
    layer_output, entry, partial = layer(lengths, own, peer, input_weight, output_weight, cot)
    every_grad = send_back(lengths, own, entry, partial, cot, user_count)
    every_item = jnp.concatenate([history_items, twin_items], axis=0)
    starts = seq_rows * jnp.stack([seq_index, 1 - seq_index])
    counts = jnp.clip(lengths[None, :] - starts[:, None], 0, seq_rows).reshape(-1)
    owned_rows = item_table.shape[1] // lax.axis_size("seq")
    table_gradient = scatter(every_item, counts, every_grad, owned_rows, seq_index)
    return (layer_output[None], table_gradient)


def solution(mesh):
    in_specs = (P(None, "seq"), P(), P("col", None), P(), P(), P("col", "seq", None))
    out_specs = (P("col", "seq", None), P("col", "seq"))
    return jax.shard_map(
        per_device, mesh=mesh, in_specs=in_specs, out_specs=out_specs, check_vma=False
    )
```

```python
import jax
import jax.numpy as jnp
from jax import lax
from jax.experimental import pallas as pl
from jax.experimental.pallas import tpu as pltpu
from jax.sharding import PartitionSpec as P

H = 8
DH = 64
LEN = 1024


norm_epsilon = 1e-05


LANES = 128
BLOCK = 256
F32 = jnp.float32
BF16 = jnp.bfloat16
MESH = pl.DeviceIdType.MESH
COPIES = 8
VMEM_BYTES = 58 * 1024 * 1024


def packed_place(items, feat):
    groups = LANES // feat
    row = (items // (LANES * groups)) * LANES + items % LANES
    slot = (items // LANES) % groups
    return row, slot


def greet_all(barrier, users, halves, me):
    def greet(other, carry):
        @pl.when(other != me)
        def _():
            pl.semaphore_signal(
                barrier, inc=1, device_id=(other // halves, other % halves), device_id_type=MESH
            )

        return carry

    lax.fori_loop(0, users * halves, greet, 0)


def lookup_kernel(
    rows_ref, slot_ref, table_ref, items_ref, own_ref, peer_ref, twin_items_ref,
    packed, picked, slab, own, peer, twin, own_sent, own_got, peer_sent, peer_got, twin_sems,
):
    feat, table_cols = table_ref.shape
    users, _, seq_rows = slot_ref.shape
    groups = LANES // feat
    span = LANES * groups
    col = lax.axis_index("col")
    seq = lax.axis_index("seq")
    barrier = pltpu.get_barrier_semaphore()
    halves = lax.axis_size("seq")

    greet_all(barrier, users, halves, col * halves + seq)

    def pack(block, carry):
        base = pl.multiple_of(block * span, span)
        parts = [table_ref[:, pl.ds(base + g * LANES, LANES)] for g in range(groups)]
        turned = jnp.concatenate(parts, axis=0).astype(BF16).T.astype(F32)
        packed[pl.ds(pl.multiple_of(block * LANES, LANES), LANES), :] = turned
        return carry

    lax.fori_loop(0, table_cols // span, pack, 0, unroll=4)
    pl.semaphore_wait(barrier, users * halves - 1)
    items_copy = pltpu.make_async_remote_copy(
        src_ref=items_ref,
        dst_ref=twin,
        send_sem=twin_sems.at[0],
        recv_sem=twin_sems.at[1],
        device_id=(col, 1 - seq),
        device_id_type=MESH,
    )
    items_copy.start()

    def to_own(user, sender):
        return pltpu.make_async_remote_copy(
            src_ref=slab.at[user],
            dst_ref=own.at[sender],
            send_sem=own_sent.at[user],
            recv_sem=own_got.at[sender],
            device_id=(user, seq),
            device_id_type=MESH,
        )

    def to_peer(user, sender):
        return pltpu.make_async_remote_copy(
            src_ref=slab.at[user],
            dst_ref=peer.at[sender],
            send_sem=peer_sent.at[user],
            recv_sem=peer_got.at[sender],
            device_id=(user, 1),
            device_id_type=MESH,
        )

    def one_user(step, carry):
        user = lax.rem(col + 1 + step, users)

        def pick(part, inner):
            base = pl.multiple_of(part * 32, 32)
            for offset in range(32):
                row = rows_ref[user, base + offset]
                picked[pl.ds(base + offset, 1), :] = packed[pl.ds(row, 1), :]
            return inner

        lax.fori_loop(0, seq_rows // 32, pick, 0)
        for part in range(seq_rows // LANES):
            turned = picked[pl.ds(part * LANES, LANES), :].astype(BF16).T.astype(F32)
            slot = slot_ref[user, :, pl.ds(part * LANES, LANES)]
            total = jnp.zeros((feat, LANES), jnp.float32)
            for g in range(groups):
                total = jnp.where(slot == g, turned[g * feat : (g + 1) * feat, :], total)
            slab[user, :, pl.ds(part * LANES, LANES)] = total.astype(slab.dtype)

        @pl.when(seq == 0)
        def _():
            to_peer(user, col).start()

        @pl.when(user != col)
        def _():
            to_own(user, col).start()

        return carry

    lax.fori_loop(0, users, one_user, 0)
    own_ref[col] = slab[col]
    items_copy.wait()
    twin_items_ref[...] = twin[...]

    def collect(step, carry):
        other = lax.rem(col + 1 + step, users)
        to_own(other, other).wait_recv()
        own_ref[other] = own[other]
        return carry

    lax.fori_loop(0, users - 1, collect, 0)

    @pl.when(seq == 1)
    def _():
        def collect_peer(other, carry):
            to_peer(other, other).wait_recv()
            return carry

        lax.fori_loop(0, users, collect_peer, 0)
        peer_ref[...] = peer[...]

    @pl.when(seq == 0)
    def _():
        peer_ref[...] = jnp.zeros_like(peer_ref)

    def sent(step, carry):
        other = lax.rem(col + 1 + step, users)
        to_own(other, col).wait_send()
        return carry

    lax.fori_loop(0, users - 1, sent, 0)

    @pl.when(seq == 0)
    def _():
        def sent_peer(other, carry):
            to_peer(other, col).wait_send()
            return carry

        lax.fori_loop(0, users, sent_peer, 0)


def lookup(items, item_table):
    feat, table_cols = item_table.shape
    users, seq_rows = items.shape
    row, slot = packed_place(items, feat)
    vmem = pl.BlockSpec(memory_space=pltpu.VMEM)
    slabs = (users, feat, seq_rows)
    return pl.pallas_call(
        lookup_kernel,
        out_shape=(jax.ShapeDtypeStruct(slabs, jnp.bfloat16),) * 2
        + (jax.ShapeDtypeStruct(items.shape, items.dtype),),
        in_specs=[pl.BlockSpec(memory_space=pltpu.SMEM), vmem, vmem, vmem],
        out_specs=(vmem,) * 3,
        scratch_shapes=[
            pltpu.VMEM((table_cols * feat // LANES, LANES), jnp.float32),
            pltpu.VMEM((seq_rows, LANES), jnp.float32),
            pltpu.VMEM(slabs, jnp.bfloat16),
            pltpu.VMEM(slabs, jnp.bfloat16),
            pltpu.VMEM(slabs, jnp.bfloat16),
            pltpu.VMEM(items.shape, items.dtype),
        ]
        + [pltpu.SemaphoreType.DMA((users,))] * 4
        + [pltpu.SemaphoreType.DMA((2,))],
        compiler_params=pltpu.CompilerParams(
            vmem_limit_bytes=VMEM_BYTES, collective_id=0, has_side_effects=True
        ),
        name="lookup",
    )(row, slot[:, None], item_table, items)


def scatter_kernel(rows_ref, count_ref, slot_ref, grad_ref, out_ref, placed, *sums):
    feat, owned = out_ref.shape
    blocks, _, seq_rows = slot_ref.shape
    groups = LANES // feat
    span = LANES * groups

    def clear(step, carry):
        at = pl.ds(pl.multiple_of(step * LANES, LANES), LANES)
        for total in sums:
            total[at, :] = jnp.zeros((LANES, LANES), jnp.float32)
        return carry

    lax.fori_loop(0, owned // span, clear, 0)

    def one_block(block, carry):
        count = count_ref[block]

        def place(part, inner):
            at = pl.ds(pl.multiple_of(part * LANES, LANES), LANES)
            grad = grad_ref[block, :, at].astype(jnp.float32)
            slot = slot_ref[block, :, at]
            spread = jnp.concatenate(
                [jnp.where(slot == g, grad, 0.0) for g in range(groups)], axis=0
            )
            placed[at, :] = spread.astype(BF16).T.astype(F32)
            return inner

        lax.fori_loop(0, (count + LANES - 1) // LANES, place, 0)

        def add(step, inner):
            base = pl.multiple_of(step * 4 * COPIES, 4 * COPIES)
            for quarter in range(4):
                first = base + quarter * COPIES
                rows = [rows_ref[block, first + n] for n in range(COPIES)]
                news = [
                    sums[n][pl.ds(rows[n], 1), :] + placed[pl.ds(first + n, 1), :]
                    for n in range(COPIES)
                ]
                for n in range(COPIES):
                    sums[n][pl.ds(rows[n], 1), :] = news[n]
            return inner

        lax.fori_loop(0, (count + 4 * COPIES - 1) // (4 * COPIES), add, 0)
        return carry

    lax.fori_loop(0, blocks, one_block, 0)

    def unpack(step, carry):
        at = pl.ds(pl.multiple_of(step * LANES, LANES), LANES)
        total = sums[0][at, :]
        for other in sums[1:]:
            total = total + other[at, :]
        turned = total.T
        base = pl.multiple_of(step * span, span)
        for g in range(groups):
            out_ref[:, pl.ds(base + g * LANES, LANES)] = turned[g * feat : (g + 1) * feat, :]
        return carry

    lax.fori_loop(0, owned // span, unpack, 0, unroll=4)


def scatter(items, counts, grads, owned, seq_index):
    feat = grads.shape[1]
    local = items % owned
    row, slot = packed_place(local, feat)
    slot = jnp.where(items // owned == seq_index, slot, -1)
    packed_rows = owned * feat // LANES
    return pl.pallas_call(
        scatter_kernel,
        out_shape=jax.ShapeDtypeStruct((feat, owned), jnp.float32),
        in_specs=[
            pl.BlockSpec(memory_space=pltpu.SMEM),
            pl.BlockSpec(memory_space=pltpu.SMEM),
            pl.BlockSpec(memory_space=pltpu.VMEM),
            pl.BlockSpec(memory_space=pltpu.VMEM),
        ],
        out_specs=pl.BlockSpec(memory_space=pltpu.VMEM),
        scratch_shapes=[pltpu.VMEM((grads.shape[2], LANES), jnp.float32)]
        + [pltpu.VMEM((packed_rows, LANES), jnp.float32)] * COPIES,
        compiler_params=pltpu.CompilerParams(vmem_limit_bytes=VMEM_BYTES),
        name="scatter",
    )(row, counts, slot[:, None], grads)


def dot(left, right):
    return jnp.dot(left, right, preferred_element_type=F32)


def dot_last(left, right):
    return lax.dot_general(left, right, (((1,), (1,)), ((), ())), preferred_element_type=F32)


def turn(block):
    return block.astype(F32).T


def column_stats(block):
    average = jnp.mean(block, axis=0, keepdims=True)
    centered = block - average
    variance = jnp.mean(centered * centered, axis=0, keepdims=True)
    return centered, lax.rsqrt(variance + norm_epsilon)


def norm_back(normed, scale, grad):
    along = jnp.mean(grad * normed, axis=0, keepdims=True)
    return scale * (grad - jnp.mean(grad, axis=0, keepdims=True) - normed * along)


def sigmoid(block):
    return 0.5 + 0.5 * jnp.tanh(0.5 * block)


def layer_kernel(
    lengths_ref, own_ref, peer_ref, in_turned_ref, in_ref, out_turned_ref, out_w_ref, cot_ref,
    out_ref, back_ref,
    normed, act, slope, act_peer, slope_peer, query_rows, att, scale, gated, grad_cols, grad_rows,
    point, bend, point_peer, bend_peer, pre_grad, pre_grad_peer, query_grad,
    entry, partial, extra, grad, mine, others, extra_sems, sent, got, passed, passed_got,
):
    hidden, rows = own_ref.shape
    users, feat, _ = grad.shape
    halves = lax.axis_size("seq")
    col = lax.axis_index("col")
    seq = lax.axis_index("seq")
    length = lengths_ref[col]
    first = seq * rows
    barrier = pltpu.get_barrier_semaphore()
    greet_all(barrier, users, halves, col * halves + seq)
    score_scale = DH ** (-0.5)
    length_scale = 1.0 / LEN
    lane_pos = lax.broadcasted_iota(jnp.int32, (1, rows), 1)
    valid = lane_pos + first < length
    valid_peer = lane_pos < length
    has_peer = seq == 1

    def normalize(ref):
        def chunk(step, carry):
            at = pl.ds(pl.multiple_of(step * LANES, LANES), LANES)
            centered, inverse = column_stats(ref[:, at].astype(F32))
            normed[:, at] = (centered * inverse).astype(BF16)
            return carry

        lax.fori_loop(0, rows // LANES, chunk, 0)

    def project(from_row, to_row, count, act_out, slope_out, keep):
        def tile(step, carry):
            source = pl.ds(pl.multiple_of(from_row + step * BLOCK, BLOCK), BLOCK)
            target = pl.ds(pl.multiple_of(to_row + step * BLOCK, BLOCK), BLOCK)
            pre = dot(in_turned_ref[source, :], normed[...])
            sig = sigmoid(pre)
            result = pre * sig
            if keep is not None:
                result = jnp.where(keep, result, 0.0)
            act_out[target, :] = result.astype(BF16)
            slope_out[target, :] = sig * (1.0 + pre * (1.0 - sig))
            return carry

        lax.fori_loop(0, count // BLOCK, tile, 0)

    normalize(own_ref)
    project(0, 0, hidden, act, slope, None)
    project(hidden, hidden, hidden, act, slope, valid)
    project(2 * hidden, 2 * hidden, 2 * hidden, act, slope, None)

    @pl.when(has_peer)
    def _():
        normalize(peer_ref)
        project(hidden, 0, hidden, act_peer, slope_peer, valid_peer)
        project(3 * hidden, hidden, hidden, act_peer, slope_peer, None)

    def head_rows(start, head):
        return pl.ds(pl.multiple_of(start + head * DH, DH), DH)

    def weigh(scores):
        scaled = scores * score_scale
        sig = sigmoid(scaled)
        silu = scaled * sig
        return silu * length_scale, (sig + silu * (1.0 - sig)) * length_scale

    below = lax.broadcasted_iota(jnp.int32, (BLOCK, BLOCK), 1) <= lax.broadcasted_iota(
        jnp.int32, (BLOCK, BLOCK), 0
    )
    blocks = rows // BLOCK

    def forward(head, carry):
        query_rows[head] = turn(act[head_rows(2 * hidden, head), :]).astype(BF16)
        for i in range(blocks):
            at_i = pl.ds(i * BLOCK, BLOCK)
            query = query_rows[head, at_i, :]
            total = jnp.zeros((DH, BLOCK), F32)
            for j in range(i + 1):
                at_j = pl.ds(j * BLOCK, BLOCK)
                weight, curve = weigh(dot(query, act[head_rows(3 * hidden, head), at_j]))
                if i == j:
                    weight = jnp.where(below, weight, 0.0)
                    curve = jnp.where(below, curve, 0.0)
                weight = weight.astype(BF16)
                point[head, at_i, at_j] = weight
                bend[head, at_i, at_j] = curve.astype(BF16)
                total += dot_last(act[head_rows(hidden, head), at_j], weight)
            att[head_rows(0, head), at_i] = total

        @pl.when(has_peer)
        def _():
            for i in range(blocks):
                at_i = pl.ds(i * BLOCK, BLOCK)
                query = query_rows[head, at_i, :]
                weight, curve = weigh(dot(query, act_peer[head_rows(hidden, head), :]))
                weight = weight.astype(BF16)
                point_peer[head, at_i, :] = weight
                bend_peer[head, at_i, :] = curve.astype(BF16)
                att[head_rows(0, head), at_i] += dot_last(act_peer[head_rows(0, head), :], weight)

        return carry

    lax.fori_loop(0, H, forward, 0)

    def gate(step, carry):
        at = pl.ds(pl.multiple_of(step * LANES, LANES), LANES)
        centered, inverse = column_stats(att[:, at])
        normed_att = centered * inverse
        att[:, at] = normed_att
        scale[:, at] = inverse
        gated[:, at] = (normed_att * act[0:hidden, at].astype(F32)).astype(BF16)
        return carry

    lax.fori_loop(0, rows // LANES, gate, 0)

    def mix(step, carry):
        at = pl.ds(pl.multiple_of(step * LANES, LANES), LANES)
        mixed = dot(out_turned_ref[...], gated[:, at]) + own_ref[:, at].astype(F32)
        base = first + step * LANES
        row_valid = lax.broadcasted_iota(jnp.int32, (LANES, hidden), 0) + base < length
        out_ref[at, :] = jnp.where(row_valid, mixed.T, 0.0).astype(BF16)
        cot = jnp.where(row_valid, cot_ref[at, :].astype(F32), 0.0).astype(BF16)
        gated_grad = dot_last(out_w_ref[...], cot)
        normed_att = att[:, at]
        pre_grad[0:hidden, at] = (gated_grad * normed_att * slope[0:hidden, at]).astype(BF16)
        normed_grad = gated_grad * act[0:hidden, at].astype(F32)
        att_grad = norm_back(normed_att, scale[:, at], normed_grad)
        grad_cols[:, at] = att_grad.astype(BF16)
        return carry

    lax.fori_loop(0, rows // LANES, mix, 0)

    def backward_peer(head, carry):
        grad_rows[head] = turn(grad_cols[head_rows(0, head), :]).astype(BF16)
        value_total = jnp.zeros((DH, rows), F32)
        key_total = jnp.zeros((DH, rows), F32)
        for i in range(blocks):
            at_i = pl.ds(i * BLOCK, BLOCK)
            weight_grad = dot(grad_rows[head, at_i, :], act_peer[head_rows(0, head), :])
            score_grad = (weight_grad * bend_peer[head, at_i, :].astype(F32)).astype(BF16)
            value_total += dot(grad_cols[head_rows(0, head), at_i], point_peer[head, at_i, :])
            key_total += dot(act[head_rows(2 * hidden, head), at_i], score_grad)
            query_grad[head_rows(0, head), at_i] = dot_last(
                act_peer[head_rows(hidden, head), :], score_grad
            )
        value_total = jnp.where(valid_peer, value_total, 0.0)
        pre_grad_peer[head_rows(0, head), :] = (
            value_total * slope_peer[head_rows(0, head), :]
        ).astype(BF16)
        pre_grad_peer[head_rows(hidden, head), :] = (
            key_total * score_scale * slope_peer[head_rows(hidden, head), :]
        ).astype(BF16)
        return carry

    def leave_peer(step, carry):
        at = pl.ds(pl.multiple_of(step * BLOCK, BLOCK), BLOCK)
        total = dot(in_ref[at, hidden : 2 * hidden], pre_grad_peer[0:hidden, :])
        total += dot(in_ref[at, 3 * hidden :], pre_grad_peer[hidden:, :])
        partial[at, :] = total.astype(BF16)
        return carry

    pl.semaphore_wait(barrier, users * halves - 1)
    extra_copy = pltpu.make_async_remote_copy(
        src_ref=partial,
        dst_ref=extra,
        send_sem=extra_sems.at[0],
        recv_sem=extra_sems.at[1],
        device_id=(col, 0),
        device_id_type=MESH,
    )

    @pl.when(has_peer)
    def _():
        lax.fori_loop(0, H, backward_peer, 0)
        lax.fori_loop(0, hidden // BLOCK, leave_peer, 0)
        extra_copy.start()
        extra[...] = jnp.zeros_like(extra)

    @pl.when(jnp.logical_not(has_peer))
    def _():
        def rows_only(head, carry):
            grad_rows[head] = turn(grad_cols[head_rows(0, head), :]).astype(BF16)
            return carry

        lax.fori_loop(0, H, rows_only, 0)
        query_grad[...] = jnp.zeros_like(query_grad)

    def backward(head, carry):
        value_parts = [jnp.zeros((DH, BLOCK), F32) for _ in range(blocks)]
        key_parts = [jnp.zeros((DH, BLOCK), F32) for _ in range(blocks)]
        for i in range(blocks):
            at_i = pl.ds(i * BLOCK, BLOCK)
            query_total = query_grad[head_rows(0, head), at_i]
            for j in range(i + 1):
                at_j = pl.ds(j * BLOCK, BLOCK)
                weight_grad = dot(grad_rows[head, at_i, :], act[head_rows(hidden, head), at_j])
                score_grad = (weight_grad * bend[head, at_i, at_j].astype(F32)).astype(BF16)
                value_parts[j] += dot(grad_cols[head_rows(0, head), at_i], point[head, at_i, at_j])
                key_parts[j] += dot(act[head_rows(2 * hidden, head), at_i], score_grad)
                query_total += dot_last(act[head_rows(3 * hidden, head), at_j], score_grad)
            query_at = head_rows(2 * hidden, head)
            pre_grad[query_at, at_i] = (query_total * score_scale * slope[query_at, at_i]).astype(
                BF16
            )
        value_total = jnp.where(valid, jnp.concatenate(value_parts, axis=1), 0.0)
        key_total = jnp.concatenate(key_parts, axis=1) * score_scale
        for start, total in ((hidden, value_total), (3 * hidden, key_total)):
            at = head_rows(start, head)
            pre_grad[at, :] = (total * slope[at, :]).astype(BF16)
        return carry

    lax.fori_loop(0, H, backward, 0)

    def leave_own(step, carry):
        at = pl.ds(pl.multiple_of(step * BLOCK, BLOCK), BLOCK)
        entry[at, :] = dot(in_ref[at, :], pre_grad[...])
        return carry

    lax.fori_loop(0, hidden // BLOCK, leave_own, 0)

    @pl.when(seq == 0)
    def _():
        extra_copy.wait_recv()

    def chunk(step, carry):
        at = pl.ds(pl.multiple_of(step * LANES, LANES), LANES)
        centered, inverse = column_stats(own_ref[:, at].astype(F32))
        received = jnp.where(seq == 0, extra[:, at].astype(F32), 0.0)
        back = norm_back(centered * inverse, inverse, entry[:, at] + received)
        lane_valid = (
            lax.broadcasted_iota(jnp.int32, (1, LANES), 1) + first + step * LANES < length
        )
        total = jnp.where(lane_valid, turn(cot_ref[at, :]), 0.0) + back
        grad[:, :, at] = total.reshape(users, feat, LANES).astype(BF16)
        return carry

    lax.fori_loop(0, rows // LANES, chunk, 0)

    def to_owner(user, sender):
        return pltpu.make_async_remote_copy(
            src_ref=grad.at[user],
            dst_ref=mine.at[sender],
            send_sem=sent.at[user],
            recv_sem=got.at[sender],
            device_id=(user, seq),
            device_id_type=MESH,
        )

    def to_twin(source, sender):
        return pltpu.make_async_remote_copy(
            src_ref=source.at[sender],
            dst_ref=others.at[sender],
            send_sem=passed.at[sender],
            recv_sem=passed_got.at[sender],
            device_id=(col, 1 - seq),
            device_id_type=MESH,
        )

    def send(step, carry):
        user = lax.rem(col + 1 + step, users)
        to_owner(user, col).start()
        return carry

    lax.fori_loop(0, users - 1, send, 0)
    to_twin(grad, col).start()
    back_ref[col] = grad[col]

    def forward(step, carry):
        sender = lax.rem(col + users - 1 - step, users)
        to_owner(sender, sender).wait_recv()
        to_twin(mine, sender).start()
        back_ref[sender] = mine[sender]
        return carry

    lax.fori_loop(0, users - 1, forward, 0)

    def collect(step, carry):
        sender = lax.rem(col + users - step, users)
        to_twin(mine, sender).wait_recv()
        back_ref[users + sender] = others[sender]
        return carry

    lax.fori_loop(0, users, collect, 0)

    def leave(step, carry):
        user = lax.rem(col + 1 + step, users)
        to_owner(user, col).wait_send()
        to_twin(mine, user).wait_send()
        return carry

    lax.fori_loop(0, users - 1, leave, 0)
    to_twin(grad, col).wait_send()

    @pl.when(seq == 1)
    def _():
        extra_copy.wait_send()


def layer(lengths, own, peer, input_weight, output_weight, cot, users):
    hidden, rows = own.shape
    slabs = (users, hidden // users, rows)
    vmem = pl.BlockSpec(memory_space=pltpu.VMEM)
    return pl.pallas_call(
        layer_kernel,
        out_shape=(
            jax.ShapeDtypeStruct((rows, hidden), BF16),
            jax.ShapeDtypeStruct((2 * users,) + slabs[1:], BF16),
        ),
        in_specs=[pl.BlockSpec(memory_space=pltpu.SMEM)] + [vmem] * 7,
        out_specs=(vmem,) * 2,
        scratch_shapes=[
            pltpu.VMEM((hidden, rows), BF16),
            pltpu.VMEM((4 * hidden, rows), BF16),
            pltpu.VMEM((4 * hidden, rows), F32),
            pltpu.VMEM((2 * hidden, rows), BF16),
            pltpu.VMEM((2 * hidden, rows), F32),
            pltpu.VMEM((H, rows, DH), BF16),
            pltpu.VMEM((hidden, rows), F32),
            pltpu.VMEM((1, rows), F32),
            pltpu.VMEM((hidden, rows), BF16),
            pltpu.VMEM((hidden, rows), BF16),
            pltpu.VMEM((H, rows, DH), BF16),
            pltpu.VMEM((H, rows, rows), BF16),
            pltpu.VMEM((H, rows, rows), BF16),
            pltpu.VMEM((H, rows, rows), BF16),
            pltpu.VMEM((H, rows, rows), BF16),
            pltpu.VMEM((4 * hidden, rows), BF16),
            pltpu.VMEM((2 * hidden, rows), BF16),
            pltpu.VMEM((hidden, rows), F32),
            pltpu.VMEM((hidden, rows), F32),
            pltpu.VMEM((hidden, rows), BF16),
            pltpu.VMEM((hidden, rows), BF16),
        ]
        + [pltpu.VMEM(slabs, BF16)] * 3
        + [pltpu.SemaphoreType.DMA((2,))]
        + [pltpu.SemaphoreType.DMA((users,))] * 4,
        compiler_params=pltpu.CompilerParams(
            vmem_limit_bytes=VMEM_BYTES, collective_id=1, has_side_effects=True
        ),
        name="layer",
    )(lengths, own, peer, input_weight.T, input_weight, output_weight.T, output_weight, cot)


def per_device(history_items, lengths, item_table, input_weight, output_weight, output_cotangent):
    user_count, seq_rows = history_items.shape
    feat_cols = item_table.shape[0]
    seq_index = lax.axis_index("seq")
    own, peer, twin_items = lookup(history_items, item_table)
    own = own.reshape(user_count * feat_cols, seq_rows)
    peer = peer.reshape(user_count * feat_cols, seq_rows)
    cot = output_cotangent[0]
    layer_output, every_grad = layer(
        lengths, own, peer, input_weight, output_weight, cot, user_count
    )
    every_item = jnp.concatenate([history_items, twin_items], axis=0)
    starts = seq_rows * jnp.stack([seq_index, 1 - seq_index])
    counts = jnp.clip(lengths[None, :] - starts[:, None], 0, seq_rows).reshape(-1)
    owned_rows = item_table.shape[1] // lax.axis_size("seq")
    table_gradient = scatter(every_item, counts, every_grad, owned_rows, seq_index)
    return (layer_output[None], table_gradient)


def solution(mesh):
    in_specs = (P(None, "seq"), P(), P("col", None), P(), P(), P("col", "seq", None))
    out_specs = (P("col", "seq", None), P("col", "seq"))
    return jax.shard_map(
        per_device, mesh=mesh, in_specs=in_specs, out_specs=out_specs, check_vma=False
    )
```

```python
import jax
import jax.numpy as jnp
from jax import lax
from jax.experimental import pallas as pl
from jax.experimental.pallas import tpu as pltpu
from jax.sharding import PartitionSpec as P

H = 8
DH = 64
LEN = 1024


norm_epsilon = 1e-05


LANES = 128
BLOCK = 256
F32 = jnp.float32
BF16 = jnp.bfloat16
MESH = pl.DeviceIdType.MESH
COPIES = 8
VMEM_BYTES = 58 * 1024 * 1024


def packed_place(items, feat):
    groups = LANES // feat
    row = ((items >> (LANES * groups).bit_length() - 1) << 7) | (items & (LANES - 1))
    slot = (items >> 7) & (groups - 1)
    return row, slot


def greet_all(barrier, users, halves, me):
    def greet(other, carry):
        @pl.when(other != me)
        def _():
            pl.semaphore_signal(
                barrier, inc=1, device_id=(other // halves, other % halves), device_id_type=MESH
            )

        return carry

    lax.fori_loop(0, users * halves, greet, 0)


def lookup_kernel(
    rows_ref, table_ref, items_ref, own_ref, peer_ref, place_ref, place_slot_ref,
    packed, picked, slot_ref, slab, own, peer, twin, own_sent, own_got, peer_sent, peer_got, twin_sems,
):
    feat, table_cols = table_ref.shape
    users, _, seq_rows = slot_ref.shape
    groups = LANES // feat
    span = LANES * groups
    col = lax.axis_index("col")
    seq = lax.axis_index("seq")
    barrier = pltpu.get_barrier_semaphore()
    halves = lax.axis_size("seq")

    greet_all(barrier, users, halves, col * halves + seq)

    def pack(block, carry):
        base = pl.multiple_of(block * span, span)
        parts = [table_ref[:, pl.ds(base + g * LANES, LANES)] for g in range(groups)]
        turned = jnp.concatenate(parts, axis=0).astype(BF16).T.astype(F32)
        packed[pl.ds(pl.multiple_of(block * LANES, LANES), LANES), :] = turned
        return carry

    lax.fori_loop(0, table_cols // span, pack, 0, unroll=4)
    _, slots = packed_place(items_ref[...], feat)
    for user in range(users):
        slot_ref[user] = slots[user : user + 1, :]
    pl.semaphore_wait(barrier, users * halves - 1)
    items_copy = pltpu.make_async_remote_copy(
        src_ref=items_ref,
        dst_ref=twin,
        send_sem=twin_sems.at[0],
        recv_sem=twin_sems.at[1],
        device_id=(col, 1 - seq),
        device_id_type=MESH,
    )
    items_copy.start()

    def to_own(user, sender):
        return pltpu.make_async_remote_copy(
            src_ref=slab.at[user],
            dst_ref=own.at[sender],
            send_sem=own_sent.at[user],
            recv_sem=own_got.at[sender],
            device_id=(user, seq),
            device_id_type=MESH,
        )

    def to_peer(source, sender):
        return pltpu.make_async_remote_copy(
            src_ref=source.at[sender],
            dst_ref=peer.at[sender],
            send_sem=peer_sent.at[sender],
            recv_sem=peer_got.at[sender],
            device_id=(col, 1),
            device_id_type=MESH,
        )

    def pass_on(step):
        sender = lax.rem(col + users - 1 - step, users)
        to_own(sender, sender).wait_recv()
        to_peer(own, sender).start()

    def one_user(step, carry):
        user = lax.rem(col + 1 + step, users)

        def pick(part, inner):
            base = pl.multiple_of(part * 32, 32)
            for offset in range(32):
                row = rows_ref[user, base + offset]
                picked[pl.ds(base + offset, 1), :] = packed[pl.ds(row, 1), :]
            return inner

        lax.fori_loop(0, seq_rows // 32, pick, 0)
        for part in range(seq_rows // LANES):
            turned = picked[pl.ds(part * LANES, LANES), :].astype(BF16).T.astype(F32)
            slot = slot_ref[user, :, pl.ds(part * LANES, LANES)]
            total = jnp.zeros((feat, LANES), jnp.float32)
            for g in range(groups):
                total = jnp.where(slot == g, turned[g * feat : (g + 1) * feat, :], total)
            slab[user, :, pl.ds(part * LANES, LANES)] = total.astype(slab.dtype)

        @pl.when(user != col)
        def _():
            to_own(user, col).start()

        @pl.when((seq == 0) & (step >= 2))
        def _():
            pass_on(step - 2)

        return carry

    lax.fori_loop(0, users, one_user, 0)

    @pl.when(seq == 0)
    def _():
        to_peer(slab, col).start()
        pass_on(users - 2)

    own_ref[col] = slab[col]
    items_copy.wait()
    owned = table_cols // halves
    for half, ref in enumerate((items_ref, twin)):
        row, slots = packed_place(ref[...] & (owned - 1), feat)
        slots = jnp.where(ref[...] >> owned.bit_length() - 1 == seq, slots, -1)
        place_ref[half * users : (half + 1) * users, :] = row
        for user in range(users):
            place_slot_ref[half * users + user] = slots[user : user + 1, :]

    def collect(step, carry):
        other = lax.rem(col + 1 + step, users)

        @pl.when(seq == 1)
        def _():
            to_own(other, other).wait_recv()

        own_ref[other] = own[other]
        return carry

    lax.fori_loop(0, users - 1, collect, 0)

    @pl.when(seq == 1)
    def _():
        def collect_peer(other, carry):
            to_peer(own, other).wait_recv()
            return carry

        lax.fori_loop(0, users, collect_peer, 0)
        peer_ref[...] = peer[...]

    @pl.when(seq == 0)
    def _():
        peer_ref[...] = jnp.zeros_like(peer_ref)

    def sent(step, carry):
        other = lax.rem(col + 1 + step, users)
        to_own(other, col).wait_send()
        return carry

    lax.fori_loop(0, users - 1, sent, 0)

    @pl.when(seq == 0)
    def _():
        def sent_peer(other, carry):
            to_peer(own, other).wait_send()
            return carry

        lax.fori_loop(0, users, sent_peer, 0)


def lookup(items, item_table):
    feat, table_cols = item_table.shape
    users, seq_rows = items.shape
    row, _ = packed_place(items, feat)
    vmem = pl.BlockSpec(memory_space=pltpu.VMEM)
    slabs = (users, feat, seq_rows)
    return pl.pallas_call(
        lookup_kernel,
        out_shape=(jax.ShapeDtypeStruct(slabs, jnp.bfloat16),) * 2
        + (
            jax.ShapeDtypeStruct((2 * users, seq_rows), jnp.int32),
            jax.ShapeDtypeStruct((2 * users, 1, seq_rows), jnp.int32),
        ),
        in_specs=[pl.BlockSpec(memory_space=pltpu.SMEM), vmem, vmem],
        out_specs=(vmem,) * 4,
        scratch_shapes=[
            pltpu.VMEM((table_cols * feat // LANES, LANES), jnp.float32),
            pltpu.VMEM((seq_rows, LANES), jnp.float32),
            pltpu.VMEM((users, 1, seq_rows), jnp.int32),
            pltpu.VMEM(slabs, jnp.bfloat16),
            pltpu.VMEM(slabs, jnp.bfloat16),
            pltpu.VMEM(slabs, jnp.bfloat16),
            pltpu.VMEM(items.shape, items.dtype),
        ]
        + [pltpu.SemaphoreType.DMA((users,))] * 4
        + [pltpu.SemaphoreType.DMA((2,))],
        compiler_params=pltpu.CompilerParams(
            vmem_limit_bytes=VMEM_BYTES, collective_id=0, has_side_effects=True
        ),
        name="lookup",
    )(row, item_table, items)


def scatter_kernel(rows_ref, lengths_ref, slot_ref, grad_ref, out_ref, placed, *sums):
    feat, owned = out_ref.shape
    blocks, _, seq_rows = slot_ref.shape
    groups = LANES // feat
    span = LANES * groups

    def clear(step, carry):
        at = pl.ds(pl.multiple_of(step * LANES, LANES), LANES)
        for total in sums:
            total[at, :] = jnp.zeros((LANES, LANES), jnp.float32)
        return carry

    lax.fori_loop(0, owned // span, clear, 0)

    def one_block(block, carry):
        users = lengths_ref.shape[0]
        seq = lax.axis_index("seq")
        start = jnp.where(block < users, seq, 1 - seq) * seq_rows
        count = jnp.clip(lengths_ref[lax.rem(block, users)] - start, 0, seq_rows)

        def place(part, inner):
            at = pl.ds(pl.multiple_of(part * LANES, LANES), LANES)
            grad = grad_ref[block, :, at].astype(jnp.float32)
            slot = slot_ref[block, :, at]
            spread = jnp.concatenate(
                [jnp.where(slot == g, grad, 0.0) for g in range(groups)], axis=0
            )
            placed[at, :] = spread.astype(BF16).T.astype(F32)
            return inner

        lax.fori_loop(0, (count + LANES - 1) // LANES, place, 0)

        def add(step, inner):
            base = pl.multiple_of(step * 4 * COPIES, 4 * COPIES)
            for quarter in range(4):
                first = base + quarter * COPIES
                rows = [rows_ref[block, first + n] for n in range(COPIES)]
                news = [
                    sums[n][pl.ds(rows[n], 1), :] + placed[pl.ds(first + n, 1), :]
                    for n in range(COPIES)
                ]
                for n in range(COPIES):
                    sums[n][pl.ds(rows[n], 1), :] = news[n]
            return inner

        lax.fori_loop(0, (count + 4 * COPIES - 1) // (4 * COPIES), add, 0)
        return carry

    lax.fori_loop(0, blocks, one_block, 0)

    def unpack(step, carry):
        at = pl.ds(pl.multiple_of(step * LANES, LANES), LANES)
        total = sums[0][at, :]
        for other in sums[1:]:
            total = total + other[at, :]
        turned = total.T
        base = pl.multiple_of(step * span, span)
        for g in range(groups):
            out_ref[:, pl.ds(base + g * LANES, LANES)] = turned[g * feat : (g + 1) * feat, :]
        return carry

    lax.fori_loop(0, owned // span, unpack, 0, unroll=4)


def scatter(row, slot, lengths, grads, owned):
    feat = grads.shape[1]
    packed_rows = owned * feat // LANES
    return pl.pallas_call(
        scatter_kernel,
        out_shape=jax.ShapeDtypeStruct((feat, owned), jnp.float32),
        in_specs=[
            pl.BlockSpec(memory_space=pltpu.SMEM),
            pl.BlockSpec(memory_space=pltpu.SMEM),
            pl.BlockSpec(memory_space=pltpu.VMEM),
            pl.BlockSpec(memory_space=pltpu.VMEM),
        ],
        out_specs=pl.BlockSpec(memory_space=pltpu.VMEM),
        scratch_shapes=[pltpu.VMEM((grads.shape[2], LANES), jnp.float32)]
        + [pltpu.VMEM((packed_rows, LANES), jnp.float32)] * COPIES,
        compiler_params=pltpu.CompilerParams(vmem_limit_bytes=VMEM_BYTES),
        name="scatter",
    )(row, lengths, slot, grads)


def dot(left, right):
    return jnp.dot(left, right, preferred_element_type=F32)


def dot_last(left, right):
    return lax.dot_general(left, right, (((1,), (1,)), ((), ())), preferred_element_type=F32)


def turn(block):
    return block.astype(F32).T


def column_stats(block):
    average = jnp.mean(block, axis=0, keepdims=True)
    centered = block - average
    variance = jnp.mean(centered * centered, axis=0, keepdims=True)
    return centered, lax.rsqrt(variance + norm_epsilon)


def norm_back(normed, scale, grad):
    along = jnp.mean(grad * normed, axis=0, keepdims=True)
    return scale * (grad - jnp.mean(grad, axis=0, keepdims=True) - normed * along)


def sigmoid(block):
    return 0.5 + 0.5 * jnp.tanh(0.5 * block)


def layer_kernel(
    lengths_ref, own_ref, peer_ref, in_turned_ref, in_ref, out_turned_ref, out_w_ref, cot_ref,
    out_ref, back_ref,
    normed, act, slope, act_peer, slope_peer, query_rows, att, scale, gated, grad_cols, grad_rows,
    point, bend, point_peer, bend_peer, pre_grad, pre_grad_peer, query_grad,
    entry, partial, extra, grad, mine, others, extra_sems, sent, got, passed, passed_got,
):
    hidden, rows = own_ref.shape
    users, feat, _ = grad.shape
    halves = lax.axis_size("seq")
    col = lax.axis_index("col")
    seq = lax.axis_index("seq")
    length = lengths_ref[col]
    first = seq * rows
    barrier = pltpu.get_barrier_semaphore()
    greet_all(barrier, users, halves, col * halves + seq)
    score_scale = DH ** (-0.5)
    length_scale = 1.0 / LEN
    lane_pos = lax.broadcasted_iota(jnp.int32, (1, rows), 1)
    valid = lane_pos + first < length
    valid_peer = lane_pos < length
    has_peer = seq == 1

    def normalize(ref):
        def chunk(step, carry):
            at = pl.ds(pl.multiple_of(step * LANES, LANES), LANES)
            centered, inverse = column_stats(ref[:, at].astype(F32))
            normed[:, at] = (centered * inverse).astype(BF16)
            return carry

        lax.fori_loop(0, rows // LANES, chunk, 0)

    def project(from_row, to_row, count, act_out, slope_out, keep):
        def tile(step, carry):
            source = pl.ds(pl.multiple_of(from_row + step * BLOCK, BLOCK), BLOCK)
            target = pl.ds(pl.multiple_of(to_row + step * BLOCK, BLOCK), BLOCK)
            pre = dot(in_turned_ref[source, :], normed[...])
            sig = sigmoid(pre)
            result = pre * sig
            if keep is not None:
                result = jnp.where(keep, result, 0.0)
            act_out[target, :] = result.astype(BF16)
            slope_out[target, :] = sig * (1.0 + pre * (1.0 - sig))
            return carry

        lax.fori_loop(0, count // BLOCK, tile, 0)

    normalize(own_ref)
    project(0, 0, hidden, act, slope, None)
    project(hidden, hidden, hidden, act, slope, valid)
    project(2 * hidden, 2 * hidden, 2 * hidden, act, slope, None)

    @pl.when(has_peer)
    def _():
        normalize(peer_ref)
        project(hidden, 0, hidden, act_peer, slope_peer, valid_peer)
        project(3 * hidden, hidden, hidden, act_peer, slope_peer, None)

    def head_rows(start, head):
        return pl.ds(pl.multiple_of(start + head * DH, DH), DH)

    def weigh(half):
        above = 1.0 + jnp.tanh(half)
        silu = half * above
        return silu, above + silu * (2.0 - above)

    below = lax.broadcasted_iota(jnp.int32, (BLOCK, BLOCK), 1) <= lax.broadcasted_iota(
        jnp.int32, (BLOCK, BLOCK), 0
    )
    blocks = rows // BLOCK

    def forward(head, carry):
        query_rows[head] = (turn(act[head_rows(2 * hidden, head), :]) * (0.5 * score_scale)).astype(BF16)
        for i in range(blocks):
            at_i = pl.ds(i * BLOCK, BLOCK)
            query = query_rows[head, at_i, :]
            total = jnp.zeros((DH, BLOCK), F32)
            for j in range(i + 1):
                at_j = pl.ds(j * BLOCK, BLOCK)
                weight, curve = weigh(dot(query, act[head_rows(3 * hidden, head), at_j]))
                if i == j:
                    weight = jnp.where(below, weight, 0.0)
                    curve = jnp.where(below, curve, 0.0)
                weight = weight.astype(BF16)
                point[head, at_i, at_j] = weight
                bend[head, at_i, at_j] = curve.astype(BF16)
                total += dot_last(act[head_rows(hidden, head), at_j], weight)
            att[head_rows(0, head), at_i] = total * length_scale

        @pl.when(has_peer)
        def _():
            for i in range(blocks):
                at_i = pl.ds(i * BLOCK, BLOCK)
                query = query_rows[head, at_i, :]
                weight, curve = weigh(dot(query, act_peer[head_rows(hidden, head), :]))
                weight = weight.astype(BF16)
                point_peer[head, at_i, :] = weight
                bend_peer[head, at_i, :] = curve.astype(BF16)
                att[head_rows(0, head), at_i] += length_scale * dot_last(
                    act_peer[head_rows(0, head), :], weight
                )

        return carry

    lax.fori_loop(0, H, forward, 0)

    def gate(step, carry):
        at = pl.ds(pl.multiple_of(step * LANES, LANES), LANES)
        centered, inverse = column_stats(att[:, at])
        normed_att = centered * inverse
        att[:, at] = normed_att
        scale[:, at] = inverse
        gated[:, at] = (normed_att * act[0:hidden, at].astype(F32)).astype(BF16)
        return carry

    lax.fori_loop(0, rows // LANES, gate, 0)

    def mix(step, carry):
        at = pl.ds(pl.multiple_of(step * LANES, LANES), LANES)
        mixed = dot(out_turned_ref[...], gated[:, at]) + own_ref[:, at].astype(F32)
        base = first + step * LANES
        row_valid = lax.broadcasted_iota(jnp.int32, (LANES, hidden), 0) + base < length
        out_ref[at, :] = jnp.where(row_valid, mixed.T, 0.0).astype(BF16)
        cot = jnp.where(row_valid, cot_ref[at, :].astype(F32), 0.0).astype(BF16)
        gated_grad = dot_last(out_w_ref[...], cot)
        normed_att = att[:, at]
        pre_grad[0:hidden, at] = (gated_grad * normed_att * slope[0:hidden, at]).astype(BF16)
        normed_grad = gated_grad * act[0:hidden, at].astype(F32)
        att_grad = norm_back(normed_att, scale[:, at], normed_grad)
        grad_cols[:, at] = att_grad.astype(BF16)
        return carry

    lax.fori_loop(0, rows // LANES, mix, 0)

    def backward_peer(head, carry):
        grad_rows[head] = (turn(grad_cols[head_rows(0, head), :]) * (0.5 * length_scale)).astype(BF16)
        value_total = jnp.zeros((DH, rows), F32)
        key_total = jnp.zeros((DH, rows), F32)
        for i in range(blocks):
            at_i = pl.ds(i * BLOCK, BLOCK)
            weight_grad = dot(grad_rows[head, at_i, :], act_peer[head_rows(0, head), :])
            score_grad = (weight_grad * bend_peer[head, at_i, :].astype(F32)).astype(BF16)
            value_total += dot(grad_cols[head_rows(0, head), at_i], point_peer[head, at_i, :])
            key_total += dot(act[head_rows(2 * hidden, head), at_i], score_grad)
            query_grad[head_rows(0, head), at_i] = dot_last(
                act_peer[head_rows(hidden, head), :], score_grad
            )
        value_total = jnp.where(valid_peer, value_total * length_scale, 0.0)
        pre_grad_peer[head_rows(0, head), :] = (
            value_total * slope_peer[head_rows(0, head), :]
        ).astype(BF16)
        pre_grad_peer[head_rows(hidden, head), :] = (
            key_total * score_scale * slope_peer[head_rows(hidden, head), :]
        ).astype(BF16)
        return carry

    def leave_peer(step, carry):
        at = pl.ds(pl.multiple_of(step * BLOCK, BLOCK), BLOCK)
        total = dot(in_ref[at, hidden : 2 * hidden], pre_grad_peer[0:hidden, :])
        total += dot(in_ref[at, 3 * hidden :], pre_grad_peer[hidden:, :])
        partial[at, :] = total.astype(BF16)
        return carry

    pl.semaphore_wait(barrier, users * halves - 1)
    extra_copy = pltpu.make_async_remote_copy(
        src_ref=partial,
        dst_ref=extra,
        send_sem=extra_sems.at[0],
        recv_sem=extra_sems.at[1],
        device_id=(col, 0),
        device_id_type=MESH,
    )

    @pl.when(has_peer)
    def _():
        lax.fori_loop(0, H, backward_peer, 0)
        lax.fori_loop(0, hidden // BLOCK, leave_peer, 0)
        extra_copy.start()
        extra[...] = jnp.zeros_like(extra)

    @pl.when(jnp.logical_not(has_peer))
    def _():
        def rows_only(head, carry):
            grad_rows[head] = (turn(grad_cols[head_rows(0, head), :]) * (0.5 * length_scale)).astype(BF16)
            return carry

        lax.fori_loop(0, H, rows_only, 0)
        query_grad[...] = jnp.zeros_like(query_grad)

    def backward(head, carry):
        value_parts = [jnp.zeros((DH, BLOCK), F32) for _ in range(blocks)]
        key_parts = [jnp.zeros((DH, BLOCK), F32) for _ in range(blocks)]
        for i in range(blocks):
            at_i = pl.ds(i * BLOCK, BLOCK)
            query_total = query_grad[head_rows(0, head), at_i]
            for j in range(i + 1):
                at_j = pl.ds(j * BLOCK, BLOCK)
                weight_grad = dot(grad_rows[head, at_i, :], act[head_rows(hidden, head), at_j])
                score_grad = (weight_grad * bend[head, at_i, at_j].astype(F32)).astype(BF16)
                value_parts[j] += dot(grad_cols[head_rows(0, head), at_i], point[head, at_i, at_j])
                key_parts[j] += dot(act[head_rows(2 * hidden, head), at_i], score_grad)
                query_total += dot_last(act[head_rows(3 * hidden, head), at_j], score_grad)
            query_at = head_rows(2 * hidden, head)
            pre_grad[query_at, at_i] = (query_total * score_scale * slope[query_at, at_i]).astype(
                BF16
            )
        value_total = jnp.where(valid, jnp.concatenate(value_parts, axis=1) * length_scale, 0.0)
        key_total = jnp.concatenate(key_parts, axis=1) * score_scale
        for start, total in ((hidden, value_total), (3 * hidden, key_total)):
            at = head_rows(start, head)
            pre_grad[at, :] = (total * slope[at, :]).astype(BF16)
        return carry

    lax.fori_loop(0, H, backward, 0)

    def leave_own(step, carry):
        at = pl.ds(pl.multiple_of(step * BLOCK, BLOCK), BLOCK)
        entry[at, :] = dot(in_ref[at, :], pre_grad[...])
        return carry

    lax.fori_loop(0, hidden // BLOCK, leave_own, 0)

    @pl.when(seq == 0)
    def _():
        extra_copy.wait_recv()

    def chunk(step, carry):
        at = pl.ds(pl.multiple_of(step * LANES, LANES), LANES)
        centered, inverse = column_stats(own_ref[:, at].astype(F32))
        received = jnp.where(seq == 0, extra[:, at].astype(F32), 0.0)
        back = norm_back(centered * inverse, inverse, entry[:, at] + received)
        lane_valid = (
            lax.broadcasted_iota(jnp.int32, (1, LANES), 1) + first + step * LANES < length
        )
        total = jnp.where(lane_valid, turn(cot_ref[at, :]), 0.0) + back
        grad[:, :, at] = total.reshape(users, feat, LANES).astype(BF16)
        return carry

    lax.fori_loop(0, rows // LANES, chunk, 0)

    def to_owner(user, sender):
        return pltpu.make_async_remote_copy(
            src_ref=grad.at[user],
            dst_ref=mine.at[sender],
            send_sem=sent.at[user],
            recv_sem=got.at[sender],
            device_id=(user, seq),
            device_id_type=MESH,
        )

    def to_twin(source, sender):
        return pltpu.make_async_remote_copy(
            src_ref=source.at[sender],
            dst_ref=others.at[sender],
            send_sem=passed.at[sender],
            recv_sem=passed_got.at[sender],
            device_id=(col, 1 - seq),
            device_id_type=MESH,
        )

    def send(step, carry):
        user = lax.rem(col + 1 + step, users)
        to_owner(user, col).start()
        return carry

    lax.fori_loop(0, users - 1, send, 0)
    to_twin(grad, col).start()
    back_ref[col] = grad[col]

    def forward(step, carry):
        sender = lax.rem(col + users - 1 - step, users)
        to_owner(sender, sender).wait_recv()
        to_twin(mine, sender).start()
        back_ref[sender] = mine[sender]
        return carry

    lax.fori_loop(0, users - 1, forward, 0)

    def collect(step, carry):
        sender = lax.rem(col + users - step, users)
        to_twin(mine, sender).wait_recv()
        back_ref[users + sender] = others[sender]
        return carry

    lax.fori_loop(0, users, collect, 0)

    def leave(step, carry):
        user = lax.rem(col + 1 + step, users)
        to_owner(user, col).wait_send()
        to_twin(mine, user).wait_send()
        return carry

    lax.fori_loop(0, users - 1, leave, 0)
    to_twin(grad, col).wait_send()

    @pl.when(seq == 1)
    def _():
        extra_copy.wait_send()


def layer(lengths, own, peer, input_weight, output_weight, cot, users):
    hidden, rows = own.shape
    slabs = (users, hidden // users, rows)
    vmem = pl.BlockSpec(memory_space=pltpu.VMEM)
    return pl.pallas_call(
        layer_kernel,
        out_shape=(
            jax.ShapeDtypeStruct((rows, hidden), BF16),
            jax.ShapeDtypeStruct((2 * users,) + slabs[1:], BF16),
        ),
        in_specs=[pl.BlockSpec(memory_space=pltpu.SMEM)] + [vmem] * 7,
        out_specs=(vmem,) * 2,
        scratch_shapes=[
            pltpu.VMEM((hidden, rows), BF16),
            pltpu.VMEM((4 * hidden, rows), BF16),
            pltpu.VMEM((4 * hidden, rows), F32),
            pltpu.VMEM((2 * hidden, rows), BF16),
            pltpu.VMEM((2 * hidden, rows), F32),
            pltpu.VMEM((H, rows, DH), BF16),
            pltpu.VMEM((hidden, rows), F32),
            pltpu.VMEM((1, rows), F32),
            pltpu.VMEM((hidden, rows), BF16),
            pltpu.VMEM((hidden, rows), BF16),
            pltpu.VMEM((H, rows, DH), BF16),
            pltpu.VMEM((H, rows, rows), BF16),
            pltpu.VMEM((H, rows, rows), BF16),
            pltpu.VMEM((H, rows, rows), BF16),
            pltpu.VMEM((H, rows, rows), BF16),
            pltpu.VMEM((4 * hidden, rows), BF16),
            pltpu.VMEM((2 * hidden, rows), BF16),
            pltpu.VMEM((hidden, rows), F32),
            pltpu.VMEM((hidden, rows), F32),
            pltpu.VMEM((hidden, rows), BF16),
            pltpu.VMEM((hidden, rows), BF16),
        ]
        + [pltpu.VMEM(slabs, BF16)] * 3
        + [pltpu.SemaphoreType.DMA((2,))]
        + [pltpu.SemaphoreType.DMA((users,))] * 4,
        compiler_params=pltpu.CompilerParams(
            vmem_limit_bytes=VMEM_BYTES, collective_id=1, has_side_effects=True
        ),
        name="layer",
    )(lengths, own, peer, input_weight.T, input_weight, output_weight.T, output_weight, cot)


def per_device(history_items, lengths, item_table, input_weight, output_weight, output_cotangent):
    user_count, seq_rows = history_items.shape
    feat_cols = item_table.shape[0]
    own, peer, row, slot = lookup(history_items, item_table)
    own = own.reshape(user_count * feat_cols, seq_rows)
    peer = peer.reshape(user_count * feat_cols, seq_rows)
    cot = output_cotangent[0]
    layer_output, every_grad = layer(
        lengths, own, peer, input_weight, output_weight, cot, user_count
    )
    owned_rows = item_table.shape[1] // lax.axis_size("seq")
    table_gradient = scatter(row, slot, lengths, every_grad, owned_rows)
    return (layer_output[None], table_gradient)


def solution(mesh):
    in_specs = (P(None, "seq"), P(), P("col", None), P(), P(), P("col", "seq", None))
    out_specs = (P("col", "seq", None), P("col", "seq"))
    return jax.shard_map(
        per_device, mesh=mesh, in_specs=in_specs, out_specs=out_specs, check_vma=False
    )
```

```python
import jax
import jax.numpy as jnp
from jax import lax
from jax.experimental import pallas as pl
from jax.experimental.pallas import tpu as pltpu
from jax.sharding import PartitionSpec as P

H = 8
DH = 64
LEN = 1024


norm_epsilon = 1e-05


LANES = 128
BLOCK = 256
F32 = jnp.float32
BF16 = jnp.bfloat16
MESH = pl.DeviceIdType.MESH
COPIES = 8
VMEM_BYTES = 58 * 1024 * 1024


def packed_place(items, feat):
    groups = LANES // feat
    row = ((items >> (LANES * groups).bit_length() - 1) << 7) | (items & (LANES - 1))
    slot = (items >> 7) & (groups - 1)
    return row, slot


def greet_all(barrier, users, halves, me):
    def greet(other, carry):
        @pl.when(other != me)
        def _():
            pl.semaphore_signal(
                barrier, inc=1, device_id=(other // halves, other % halves), device_id_type=MESH
            )

        return carry

    lax.fori_loop(0, users * halves, greet, 0)


def lookup_kernel(
    rows_ref, table_ref, items_ref, own_ref, peer_ref, place_ref, place_slot_ref,
    packed, picked, slot_ref, slab, own, peer, twin, own_sent, own_got, peer_sent, peer_got, twin_sems,
):
    feat, table_cols = table_ref.shape
    users, _, seq_rows = slot_ref.shape
    groups = LANES // feat
    span = LANES * groups
    col = lax.axis_index("col")
    seq = lax.axis_index("seq")
    barrier = pltpu.get_barrier_semaphore()
    halves = lax.axis_size("seq")

    greet_all(barrier, users, halves, col * halves + seq)

    def pack(block, carry):
        base = pl.multiple_of(block * span, span)
        parts = [table_ref[:, pl.ds(base + g * LANES, LANES)] for g in range(groups)]
        turned = jnp.concatenate(parts, axis=0).astype(BF16).T.astype(F32)
        packed[pl.ds(pl.multiple_of(block * LANES, LANES), LANES), :] = turned
        return carry

    lax.fori_loop(0, table_cols // span, pack, 0, unroll=4)
    _, slots = packed_place(items_ref[...], feat)
    for user in range(users):
        slot_ref[user] = slots[user : user + 1, :]
    pl.semaphore_wait(barrier, users * halves - 1)
    items_copy = pltpu.make_async_remote_copy(
        src_ref=items_ref,
        dst_ref=twin,
        send_sem=twin_sems.at[0],
        recv_sem=twin_sems.at[1],
        device_id=(col, 1 - seq),
        device_id_type=MESH,
    )
    items_copy.start()

    def to_own(user, sender):
        return pltpu.make_async_remote_copy(
            src_ref=slab.at[user],
            dst_ref=own.at[sender],
            send_sem=own_sent.at[user],
            recv_sem=own_got.at[sender],
            device_id=(user, seq),
            device_id_type=MESH,
        )

    def to_peer(source, sender):
        return pltpu.make_async_remote_copy(
            src_ref=source.at[sender],
            dst_ref=peer.at[sender],
            send_sem=peer_sent.at[sender],
            recv_sem=peer_got.at[sender],
            device_id=(col, 1),
            device_id_type=MESH,
        )

    def pass_on(step):
        sender = lax.rem(col + users - 1 - step, users)
        to_own(sender, sender).wait_recv()
        to_peer(own, sender).start()

    def one_user(step, carry):
        user = lax.rem(col + 1 + step, users)

        def pick(part, inner):
            base = pl.multiple_of(part * 32, 32)
            for offset in range(32):
                row = rows_ref[user, base + offset]
                picked[pl.ds(base + offset, 1), :] = packed[pl.ds(row, 1), :]
            return inner

        lax.fori_loop(0, seq_rows // 32, pick, 0)
        for part in range(seq_rows // LANES):
            turned = picked[pl.ds(part * LANES, LANES), :].astype(BF16).T.astype(F32)
            slot = slot_ref[user, :, pl.ds(part * LANES, LANES)]
            total = jnp.zeros((feat, LANES), jnp.float32)
            for g in range(groups):
                total = jnp.where(slot == g, turned[g * feat : (g + 1) * feat, :], total)
            slab[user, :, pl.ds(part * LANES, LANES)] = total.astype(slab.dtype)

        @pl.when(user != col)
        def _():
            to_own(user, col).start()

        @pl.when((seq == 0) & (step >= 2))
        def _():
            pass_on(step - 2)

        return carry

    lax.fori_loop(0, users, one_user, 0)

    @pl.when(seq == 0)
    def _():
        to_peer(slab, col).start()
        pass_on(users - 2)

    own_ref[col] = slab[col]
    items_copy.wait()
    owned = table_cols // halves
    for half, ref in enumerate((items_ref, twin)):
        row, slots = packed_place(ref[...] & (owned - 1), feat)
        slots = jnp.where(ref[...] >> owned.bit_length() - 1 == seq, slots, -1)
        place_ref[half * users : (half + 1) * users, :] = row
        for user in range(users):
            place_slot_ref[half * users + user] = slots[user : user + 1, :]

    def collect(step, carry):
        other = lax.rem(col + 1 + step, users)

        @pl.when(seq == 1)
        def _():
            to_own(other, other).wait_recv()

        own_ref[other] = own[other]
        return carry

    lax.fori_loop(0, users - 1, collect, 0)

    @pl.when(seq == 1)
    def _():
        def collect_peer(other, carry):
            to_peer(own, other).wait_recv()
            return carry

        lax.fori_loop(0, users, collect_peer, 0)
        peer_ref[...] = peer[...]

    @pl.when(seq == 0)
    def _():
        peer_ref[...] = jnp.zeros_like(peer_ref)

    def sent(step, carry):
        other = lax.rem(col + 1 + step, users)
        to_own(other, col).wait_send()
        return carry

    lax.fori_loop(0, users - 1, sent, 0)

    @pl.when(seq == 0)
    def _():
        def sent_peer(other, carry):
            to_peer(own, other).wait_send()
            return carry

        lax.fori_loop(0, users, sent_peer, 0)


def lookup(items, item_table):
    feat, table_cols = item_table.shape
    users, seq_rows = items.shape
    row, _ = packed_place(items, feat)
    vmem = pl.BlockSpec(memory_space=pltpu.VMEM)
    slabs = (users, feat, seq_rows)
    return pl.pallas_call(
        lookup_kernel,
        out_shape=(jax.ShapeDtypeStruct(slabs, jnp.bfloat16),) * 2
        + (
            jax.ShapeDtypeStruct((2 * users, seq_rows), jnp.int32),
            jax.ShapeDtypeStruct((2 * users, 1, seq_rows), jnp.int32),
        ),
        in_specs=[pl.BlockSpec(memory_space=pltpu.SMEM), vmem, vmem],
        out_specs=(vmem,) * 4,
        scratch_shapes=[
            pltpu.VMEM((table_cols * feat // LANES, LANES), jnp.float32),
            pltpu.VMEM((seq_rows, LANES), jnp.float32),
            pltpu.VMEM((users, 1, seq_rows), jnp.int32),
            pltpu.VMEM(slabs, jnp.bfloat16),
            pltpu.VMEM(slabs, jnp.bfloat16),
            pltpu.VMEM(slabs, jnp.bfloat16),
            pltpu.VMEM(items.shape, items.dtype),
        ]
        + [pltpu.SemaphoreType.DMA((users,))] * 4
        + [pltpu.SemaphoreType.DMA((2,))],
        compiler_params=pltpu.CompilerParams(
            vmem_limit_bytes=VMEM_BYTES, collective_id=0, has_side_effects=True
        ),
        name="lookup",
    )(row, item_table, items)


def scatter_kernel(rows_ref, lengths_ref, slot_ref, grad_ref, out_ref, placed, *sums):
    feat, owned = out_ref.shape
    blocks, _, seq_rows = slot_ref.shape
    groups = LANES // feat
    span = LANES * groups

    def clear(step, carry):
        at = pl.ds(pl.multiple_of(step * LANES, LANES), LANES)
        for total in sums:
            total[at, :] = jnp.zeros((LANES, LANES), jnp.float32)
        return carry

    lax.fori_loop(0, owned // span, clear, 0)

    def one_block(block, carry):
        users = lengths_ref.shape[0]
        seq = lax.axis_index("seq")
        start = jnp.where(block < users, seq, 1 - seq) * seq_rows
        count = jnp.clip(lengths_ref[lax.rem(block, users)] - start, 0, seq_rows)

        def place(part, inner):
            at = pl.ds(pl.multiple_of(part * LANES, LANES), LANES)
            grad = grad_ref[block, :, at].astype(jnp.float32)
            slot = slot_ref[block, :, at]
            spread = jnp.concatenate(
                [jnp.where(slot == g, grad, 0.0) for g in range(groups)], axis=0
            )
            placed[at, :] = spread.astype(BF16).T.astype(F32)
            return inner

        lax.fori_loop(0, (count + LANES - 1) // LANES, place, 0)

        def add(step, inner):
            base = pl.multiple_of(step * 4 * COPIES, 4 * COPIES)
            for quarter in range(4):
                first = base + quarter * COPIES
                rows = [rows_ref[block, first + n] for n in range(COPIES)]
                news = [
                    sums[n][pl.ds(rows[n], 1), :] + placed[pl.ds(first + n, 1), :]
                    for n in range(COPIES)
                ]
                for n in range(COPIES):
                    sums[n][pl.ds(rows[n], 1), :] = news[n]
            return inner

        lax.fori_loop(0, (count + 4 * COPIES - 1) // (4 * COPIES), add, 0)
        return carry

    lax.fori_loop(0, blocks, one_block, 0)

    def unpack(step, carry):
        at = pl.ds(pl.multiple_of(step * LANES, LANES), LANES)
        total = sums[0][at, :]
        for other in sums[1:]:
            total = total + other[at, :]
        turned = total.T
        base = pl.multiple_of(step * span, span)
        for g in range(groups):
            out_ref[:, pl.ds(base + g * LANES, LANES)] = turned[g * feat : (g + 1) * feat, :]
        return carry

    lax.fori_loop(0, owned // span, unpack, 0, unroll=4)


def scatter(row, slot, lengths, grads, owned):
    feat = grads.shape[1]
    packed_rows = owned * feat // LANES
    return pl.pallas_call(
        scatter_kernel,
        out_shape=jax.ShapeDtypeStruct((feat, owned), jnp.float32),
        in_specs=[
            pl.BlockSpec(memory_space=pltpu.SMEM),
            pl.BlockSpec(memory_space=pltpu.SMEM),
            pl.BlockSpec(memory_space=pltpu.VMEM),
            pl.BlockSpec(memory_space=pltpu.VMEM),
        ],
        out_specs=pl.BlockSpec(memory_space=pltpu.VMEM),
        scratch_shapes=[pltpu.VMEM((grads.shape[2], LANES), jnp.float32)]
        + [pltpu.VMEM((packed_rows, LANES), jnp.float32)] * COPIES,
        compiler_params=pltpu.CompilerParams(vmem_limit_bytes=VMEM_BYTES),
        name="scatter",
    )(row, lengths, slot, grads)


def dot(left, right):
    return jnp.dot(left, right, preferred_element_type=F32)


def dot_last(left, right):
    return lax.dot_general(left, right, (((1,), (1,)), ((), ())), preferred_element_type=F32)


def turn(block):
    return block.astype(F32).T


def column_stats(block):
    average = jnp.mean(block, axis=0, keepdims=True)
    centered = block - average
    variance = jnp.mean(centered * centered, axis=0, keepdims=True)
    return centered, lax.rsqrt(variance + norm_epsilon)


def norm_back(normed, scale, grad):
    along = jnp.mean(grad * normed, axis=0, keepdims=True)
    return scale * (grad - jnp.mean(grad, axis=0, keepdims=True) - normed * along)


def sigmoid(block):
    return 0.5 + 0.5 * jnp.tanh(0.5 * block)


def layer_kernel(
    lengths_ref, own_ref, peer_ref, in_ref, out_turned_ref, out_w_ref, cot_ref,
    out_ref, back_ref,
    normed, act, slope, act_peer, slope_peer, query_rows, att, scale, gated, grad_cols, grad_rows,
    point, bend, point_peer, bend_peer, pre_grad, pre_grad_peer, query_grad,
    entry, partial, extra, grad, mine, others, extra_sems, sent, got, passed, passed_got,
):
    hidden, rows = own_ref.shape
    users, feat, _ = grad.shape
    halves = lax.axis_size("seq")
    col = lax.axis_index("col")
    seq = lax.axis_index("seq")
    length = lengths_ref[col]
    first = seq * rows
    barrier = pltpu.get_barrier_semaphore()
    greet_all(barrier, users, halves, col * halves + seq)
    score_scale = DH ** (-0.5)
    length_scale = 1.0 / LEN
    lane_pos = lax.broadcasted_iota(jnp.int32, (1, rows), 1)
    valid = lane_pos + first < length
    valid_peer = lane_pos < length
    has_peer = seq == 1

    def normalize(ref):
        def chunk(step, carry):
            at = pl.ds(pl.multiple_of(step * LANES, LANES), LANES)
            centered, inverse = column_stats(ref[:, at].astype(F32))
            normed[:, at] = (centered * inverse).astype(BF16)
            return carry

        lax.fori_loop(0, rows // LANES, chunk, 0)

    def project(from_row, to_row, count, act_out, slope_out, keep):
        def tile(step, carry):
            source = pl.ds(pl.multiple_of(from_row + step * BLOCK, BLOCK), BLOCK)
            target = pl.ds(pl.multiple_of(to_row + step * BLOCK, BLOCK), BLOCK)
            pre = lax.dot_general(
                in_ref[:, source], normed[...], (((0,), (0,)), ((), ())), preferred_element_type=F32
            )
            sig = sigmoid(pre)
            result = pre * sig
            if keep is not None:
                result = jnp.where(keep, result, 0.0)
            act_out[target, :] = result.astype(BF16)
            slope_out[target, :] = sig * (1.0 + pre * (1.0 - sig))
            return carry

        lax.fori_loop(0, count // BLOCK, tile, 0)

    normalize(own_ref)
    project(0, 0, hidden, act, slope, None)
    project(hidden, hidden, hidden, act, slope, valid)
    project(2 * hidden, 2 * hidden, 2 * hidden, act, slope, None)

    @pl.when(has_peer)
    def _():
        normalize(peer_ref)
        project(hidden, 0, hidden, act_peer, slope_peer, valid_peer)
        project(3 * hidden, hidden, hidden, act_peer, slope_peer, None)

    def head_rows(start, head):
        return pl.ds(pl.multiple_of(start + head * DH, DH), DH)

    def weigh(half):
        above = 1.0 + jnp.tanh(half)
        silu = half * above
        return silu, above + silu * (2.0 - above)

    below = lax.broadcasted_iota(jnp.int32, (BLOCK, BLOCK), 1) <= lax.broadcasted_iota(
        jnp.int32, (BLOCK, BLOCK), 0
    )
    blocks = rows // BLOCK

    def forward(head, carry):
        query_rows[head] = (turn(act[head_rows(2 * hidden, head), :]) * (0.5 * score_scale)).astype(BF16)
        for i in range(blocks):
            at_i = pl.ds(i * BLOCK, BLOCK)
            query = query_rows[head, at_i, :]
            total = jnp.zeros((DH, BLOCK), F32)
            for j in range(i + 1):
                at_j = pl.ds(j * BLOCK, BLOCK)
                weight, curve = weigh(dot(query, act[head_rows(3 * hidden, head), at_j]))
                if i == j:
                    weight = jnp.where(below, weight, 0.0)
                    curve = jnp.where(below, curve, 0.0)
                weight = weight.astype(BF16)
                point[head, at_i, at_j] = weight
                bend[head, at_i, at_j] = curve.astype(BF16)
                total += dot_last(act[head_rows(hidden, head), at_j], weight)
            att[head_rows(0, head), at_i] = total * length_scale

        @pl.when(has_peer)
        def _():
            for i in range(blocks):
                at_i = pl.ds(i * BLOCK, BLOCK)
                query = query_rows[head, at_i, :]
                weight, curve = weigh(dot(query, act_peer[head_rows(hidden, head), :]))
                weight = weight.astype(BF16)
                point_peer[head, at_i, :] = weight
                bend_peer[head, at_i, :] = curve.astype(BF16)
                att[head_rows(0, head), at_i] += length_scale * dot_last(
                    act_peer[head_rows(0, head), :], weight
                )

        return carry

    lax.fori_loop(0, H, forward, 0)

    def gate(step, carry):
        at = pl.ds(pl.multiple_of(step * LANES, LANES), LANES)
        centered, inverse = column_stats(att[:, at])
        normed_att = centered * inverse
        att[:, at] = normed_att
        scale[:, at] = inverse
        gated[:, at] = (normed_att * act[0:hidden, at].astype(F32)).astype(BF16)
        return carry

    lax.fori_loop(0, rows // LANES, gate, 0)

    def mix(step, carry):
        at = pl.ds(pl.multiple_of(step * LANES, LANES), LANES)
        mixed = dot(out_turned_ref[...], gated[:, at]) + own_ref[:, at].astype(F32)
        base = first + step * LANES
        row_valid = lax.broadcasted_iota(jnp.int32, (LANES, hidden), 0) + base < length
        out_ref[at, :] = jnp.where(row_valid, mixed.T, 0.0).astype(BF16)
        cot = jnp.where(row_valid, cot_ref[at, :].astype(F32), 0.0).astype(BF16)
        gated_grad = dot_last(out_w_ref[...], cot)
        normed_att = att[:, at]
        pre_grad[0:hidden, at] = (gated_grad * normed_att * slope[0:hidden, at]).astype(BF16)
        normed_grad = gated_grad * act[0:hidden, at].astype(F32)
        att_grad = norm_back(normed_att, scale[:, at], normed_grad)
        grad_cols[:, at] = att_grad.astype(BF16)
        return carry

    lax.fori_loop(0, rows // LANES, mix, 0)

    def backward_peer(head, carry):
        grad_rows[head] = (turn(grad_cols[head_rows(0, head), :]) * (0.5 * length_scale)).astype(BF16)
        value_total = jnp.zeros((DH, rows), F32)
        key_total = jnp.zeros((DH, rows), F32)
        for i in range(blocks):
            at_i = pl.ds(i * BLOCK, BLOCK)
            weight_grad = dot(grad_rows[head, at_i, :], act_peer[head_rows(0, head), :])
            score_grad = (weight_grad * bend_peer[head, at_i, :].astype(F32)).astype(BF16)
            value_total += dot(grad_cols[head_rows(0, head), at_i], point_peer[head, at_i, :])
            key_total += dot(act[head_rows(2 * hidden, head), at_i], score_grad)
            query_grad[head_rows(0, head), at_i] = dot_last(
                act_peer[head_rows(hidden, head), :], score_grad
            )
        value_total = jnp.where(valid_peer, value_total * length_scale, 0.0)
        pre_grad_peer[head_rows(0, head), :] = (
            value_total * slope_peer[head_rows(0, head), :]
        ).astype(BF16)
        pre_grad_peer[head_rows(hidden, head), :] = (
            key_total * score_scale * slope_peer[head_rows(hidden, head), :]
        ).astype(BF16)
        return carry

    def leave_peer(step, carry):
        at = pl.ds(pl.multiple_of(step * BLOCK, BLOCK), BLOCK)
        total = dot(in_ref[at, hidden : 2 * hidden], pre_grad_peer[0:hidden, :])
        total += dot(in_ref[at, 3 * hidden :], pre_grad_peer[hidden:, :])
        partial[at, :] = total.astype(BF16)
        return carry

    pl.semaphore_wait(barrier, users * halves - 1)
    extra_copy = pltpu.make_async_remote_copy(
        src_ref=partial,
        dst_ref=extra,
        send_sem=extra_sems.at[0],
        recv_sem=extra_sems.at[1],
        device_id=(col, 0),
        device_id_type=MESH,
    )

    @pl.when(has_peer)
    def _():
        lax.fori_loop(0, H, backward_peer, 0)
        lax.fori_loop(0, hidden // BLOCK, leave_peer, 0)
        extra_copy.start()
        extra[...] = jnp.zeros_like(extra)

    @pl.when(jnp.logical_not(has_peer))
    def _():
        def rows_only(head, carry):
            grad_rows[head] = (turn(grad_cols[head_rows(0, head), :]) * (0.5 * length_scale)).astype(BF16)
            return carry

        lax.fori_loop(0, H, rows_only, 0)
        query_grad[...] = jnp.zeros_like(query_grad)

    def backward(head, carry):
        value_parts = [jnp.zeros((DH, BLOCK), F32) for _ in range(blocks)]
        key_parts = [jnp.zeros((DH, BLOCK), F32) for _ in range(blocks)]
        for i in range(blocks):
            at_i = pl.ds(i * BLOCK, BLOCK)
            query_total = query_grad[head_rows(0, head), at_i]
            for j in range(i + 1):
                at_j = pl.ds(j * BLOCK, BLOCK)
                weight_grad = dot(grad_rows[head, at_i, :], act[head_rows(hidden, head), at_j])
                score_grad = (weight_grad * bend[head, at_i, at_j].astype(F32)).astype(BF16)
                value_parts[j] += dot(grad_cols[head_rows(0, head), at_i], point[head, at_i, at_j])
                key_parts[j] += dot(act[head_rows(2 * hidden, head), at_i], score_grad)
                query_total += dot_last(act[head_rows(3 * hidden, head), at_j], score_grad)
            query_at = head_rows(2 * hidden, head)
            pre_grad[query_at, at_i] = (query_total * score_scale * slope[query_at, at_i]).astype(
                BF16
            )
        value_total = jnp.where(valid, jnp.concatenate(value_parts, axis=1) * length_scale, 0.0)
        key_total = jnp.concatenate(key_parts, axis=1) * score_scale
        for start, total in ((hidden, value_total), (3 * hidden, key_total)):
            at = head_rows(start, head)
            pre_grad[at, :] = (total * slope[at, :]).astype(BF16)
        return carry

    lax.fori_loop(0, H, backward, 0)

    def leave_own(step, carry):
        at = pl.ds(pl.multiple_of(step * BLOCK, BLOCK), BLOCK)
        entry[at, :] = dot(in_ref[at, :], pre_grad[...])
        return carry

    lax.fori_loop(0, hidden // BLOCK, leave_own, 0)

    @pl.when(seq == 0)
    def _():
        extra_copy.wait_recv()

    def chunk(step, carry):
        at = pl.ds(pl.multiple_of(step * LANES, LANES), LANES)
        centered, inverse = column_stats(own_ref[:, at].astype(F32))
        received = jnp.where(seq == 0, extra[:, at].astype(F32), 0.0)
        back = norm_back(centered * inverse, inverse, entry[:, at] + received)
        lane_valid = (
            lax.broadcasted_iota(jnp.int32, (1, LANES), 1) + first + step * LANES < length
        )
        total = jnp.where(lane_valid, turn(cot_ref[at, :]), 0.0) + back
        grad[:, :, at] = total.reshape(users, feat, LANES).astype(BF16)
        return carry

    lax.fori_loop(0, rows // LANES, chunk, 0)

    def to_owner(user, sender):
        return pltpu.make_async_remote_copy(
            src_ref=grad.at[user],
            dst_ref=mine.at[sender],
            send_sem=sent.at[user],
            recv_sem=got.at[sender],
            device_id=(user, seq),
            device_id_type=MESH,
        )

    def to_twin(source, sender):
        return pltpu.make_async_remote_copy(
            src_ref=source.at[sender],
            dst_ref=others.at[sender],
            send_sem=passed.at[sender],
            recv_sem=passed_got.at[sender],
            device_id=(col, 1 - seq),
            device_id_type=MESH,
        )

    def send(step, carry):
        user = lax.rem(col + 1 + step, users)
        to_owner(user, col).start()
        return carry

    lax.fori_loop(0, users - 1, send, 0)
    to_twin(grad, col).start()
    back_ref[col] = grad[col]

    def forward(step, carry):
        sender = lax.rem(col + users - 1 - step, users)
        to_owner(sender, sender).wait_recv()
        to_twin(mine, sender).start()
        back_ref[sender] = mine[sender]
        return carry

    lax.fori_loop(0, users - 1, forward, 0)

    def collect(step, carry):
        sender = lax.rem(col + users - step, users)
        to_twin(mine, sender).wait_recv()
        back_ref[users + sender] = others[sender]
        return carry

    lax.fori_loop(0, users, collect, 0)

    def leave(step, carry):
        user = lax.rem(col + 1 + step, users)
        to_owner(user, col).wait_send()
        to_twin(mine, user).wait_send()
        return carry

    lax.fori_loop(0, users - 1, leave, 0)
    to_twin(grad, col).wait_send()

    @pl.when(seq == 1)
    def _():
        extra_copy.wait_send()


def layer(lengths, own, peer, input_weight, output_weight, cot, users):
    hidden, rows = own.shape
    slabs = (users, hidden // users, rows)
    vmem = pl.BlockSpec(memory_space=pltpu.VMEM)
    return pl.pallas_call(
        layer_kernel,
        out_shape=(
            jax.ShapeDtypeStruct((rows, hidden), BF16),
            jax.ShapeDtypeStruct((2 * users,) + slabs[1:], BF16),
        ),
        in_specs=[pl.BlockSpec(memory_space=pltpu.SMEM)] + [vmem] * 6,
        out_specs=(vmem,) * 2,
        scratch_shapes=[
            pltpu.VMEM((hidden, rows), BF16),
            pltpu.VMEM((4 * hidden, rows), BF16),
            pltpu.VMEM((4 * hidden, rows), F32),
            pltpu.VMEM((2 * hidden, rows), BF16),
            pltpu.VMEM((2 * hidden, rows), F32),
            pltpu.VMEM((H, rows, DH), BF16),
            pltpu.VMEM((hidden, rows), F32),
            pltpu.VMEM((1, rows), F32),
            pltpu.VMEM((hidden, rows), BF16),
            pltpu.VMEM((hidden, rows), BF16),
            pltpu.VMEM((H, rows, DH), BF16),
            pltpu.VMEM((H, rows, rows), BF16),
            pltpu.VMEM((H, rows, rows), BF16),
            pltpu.VMEM((H, rows, rows), BF16),
            pltpu.VMEM((H, rows, rows), BF16),
            pltpu.VMEM((4 * hidden, rows), BF16),
            pltpu.VMEM((2 * hidden, rows), BF16),
            pltpu.VMEM((hidden, rows), F32),
            pltpu.VMEM((hidden, rows), F32),
            pltpu.VMEM((hidden, rows), BF16),
            pltpu.VMEM((hidden, rows), BF16),
        ]
        + [pltpu.VMEM(slabs, BF16)] * 3
        + [pltpu.SemaphoreType.DMA((2,))]
        + [pltpu.SemaphoreType.DMA((users,))] * 4,
        compiler_params=pltpu.CompilerParams(
            vmem_limit_bytes=VMEM_BYTES, collective_id=1, has_side_effects=True
        ),
        name="layer",
    )(lengths, own, peer, input_weight, output_weight.T, output_weight, cot)


def per_device(history_items, lengths, item_table, input_weight, output_weight, output_cotangent):
    user_count, seq_rows = history_items.shape
    feat_cols = item_table.shape[0]
    own, peer, row, slot = lookup(history_items, item_table)
    own = own.reshape(user_count * feat_cols, seq_rows)
    peer = peer.reshape(user_count * feat_cols, seq_rows)
    cot = output_cotangent[0]
    layer_output, every_grad = layer(
        lengths, own, peer, input_weight, output_weight, cot, user_count
    )
    owned_rows = item_table.shape[1] // lax.axis_size("seq")
    table_gradient = scatter(row, slot, lengths, every_grad, owned_rows)
    return (layer_output[None], table_gradient)


def solution(mesh):
    in_specs = (P(None, "seq"), P(), P("col", None), P(), P(), P("col", "seq", None))
    out_specs = (P("col", "seq", None), P("col", "seq"))
    return jax.shard_map(
        per_device, mesh=mesh, in_specs=in_specs, out_specs=out_specs, check_vma=False
    )
```
